32 devices in a mesh: row: 4 (over y, x), col: 2 (over core), depth: 4 (over z).
Axes of the slice: x: 2, y: 2, z: 4, core: 2. Of those that a mesh axis runs over, the one named last changes fastest.
Arguments:
- x_vals: bfloat16 [4, 16, 4, 128, 128], P('row', ('col', 'depth')), may hold values from -2.5 to 2.5
- x_rows: int32 [4, 16, 4], P('row', ('col', 'depth')), may hold values from -1 to 3, as said below
- out_block: int32 [4, 2, 4], P('row', 'col', 'depth'), may hold values from 0 to 15, as said below
Outputs:
- product_blocks: bfloat16 [4, 2, 4, 128, 128], P('row', 'col', 'depth')
The draws below stay inside these ranges and needn't reach their ends.
Inputs may be any that keep to these rules, and one draw needn't show every extreme that they name: `x_rows`: within one row group and block column the filled slots name distinct rows. In every row group, each run of 2 block columns that starts at a multiple of 2 has a column with all 4 slots filled. `out_block`: within one tile the 4 entries are distinct positions, and every tile lists position 15 among them.
All inputs are finite; a program needn't handle non-finite values.
Results may differ from the reference program's by a relative error of at most 0.001.
Values may be sent and summed in bfloat16 or wider, within the bound.
A program may use at most 128 MiB of HBM per device.

```python
import jax
import jax.numpy as jnp
from jax import lax

BS = 128
PW = 2
H = 4
NB = 16
RG = 4
OG = 4
N_ROW = 4
N_COL = 2


def draw_x_rows(key, part):
    cell_count = N_ROW * NB
    key_order, key_force, key_count = jax.random.split(key, 3)
    spread = jnp.arange(RG, dtype=jnp.int32)
    scores = jax.random.randint(key_order, (cell_count, RG), 0, 1 << 16, dtype=jnp.int32) * RG + spread[None, :]
    chosen_col = jax.random.randint(key_force, (N_ROW, NB // PW), 0, PW, dtype=jnp.int32)
    column = jnp.arange(NB, dtype=jnp.int32)
    forced = column[None, :] % PW == jnp.repeat(chosen_col, PW, axis=1)
    forced = forced.reshape(cell_count)
    ranking = jnp.argsort(scores, axis=1)[:, :H].astype(jnp.int32)
    counts = jax.random.randint(key_count, (cell_count,), 0, H + 1, dtype=jnp.int32)
    counts = jnp.where(forced, H, counts)
    slot_index = jnp.arange(H, dtype=jnp.int32)
    row_ids = jnp.where(slot_index[None, :] < counts[:, None], ranking, -1)
    return row_ids.reshape(N_ROW, NB, H)


def draw_out_block(key, part):
    tile_count = N_ROW * N_COL
    span_size = RG * RG
    key_pick, key_mix = jax.random.split(key, 2)
    spread = jnp.arange(span_size, dtype=jnp.int32)
    scores = jax.random.randint(key_pick, (tile_count, span_size), 0, 1 << 16, dtype=jnp.int32) * span_size + spread[None, :]
    scores = jnp.where(spread[None, :] == span_size - 1, -1, scores)
    chosen = jnp.argsort(scores, axis=1)[:, :OG].astype(jnp.int32)
    entry_spread = jnp.arange(OG, dtype=jnp.int32)
    mixing = jax.random.randint(key_mix, (tile_count, OG), 0, 1 << 16, dtype=jnp.int32) * OG + entry_spread[None, :]
    mixing = jnp.argsort(mixing, axis=1).astype(jnp.int32)
    chosen = jnp.take_along_axis(chosen, mixing, axis=1)
    return chosen.reshape(N_ROW, N_COL, OG)


def block_levels(key, shape, cuts, least, top_value):
    def one(position, parts):
        heights = jax.random.uniform(jax.random.fold_in(jax.random.fold_in(key, 6), position), (parts,), jnp.float32, least / len(cuts), top_value / len(cuts))
        return jnp.repeat(jnp.exp(heights), shape[position] // parts).reshape((-1,) + (1,) * (len(shape) - position - 1))

    loudness = one(*cuts[0])
    for cut in cuts[1:]:
        loudness = loudness * one(*cut)
    return loudness


def gaussian(own_key, extent, scale, reach, shards=(), kind=jnp.bfloat16):
    gain = block_levels(own_key, extent, shards, -0.22, 0.18) if shards else 1.0
    drawn = jax.random.normal(own_key, extent, jnp.float32) * scale * gain
    return jnp.minimum(jnp.maximum(drawn, -reach), reach).astype(kind)


def setup_inputs(seed: int = 0) -> dict:
    key_of = jax.random.split(jax.random.key(seed), 4)
    return {
        "x_vals": gaussian(key_of[0], (N_ROW, NB, H, BS, BS), 0.18, 2.5, ((0, 4), (1, 8))),
        "x_rows": draw_x_rows(jax.random.fold_in(key_of[3], 71), 0),
        "out_block": draw_out_block(jax.random.fold_in(key_of[3], 71), 0),
    }


def tile_sum(left_vals, left_rows, right_vals, right_rows, positions):
    partial_value = jnp.zeros((positions.shape[0], left_vals.shape[2], left_vals.shape[3]), jnp.float32)
    slot_total = left_vals.shape[0] * left_vals.shape[1]
    left_valid = left_rows >= 0
    left_wide = left_vals.astype(jnp.float32)
    for slot_index in range(right_vals.shape[1]):
        partner_slot = right_vals[:, slot_index].astype(jnp.float32)
        right_slot_rows = right_rows[:, slot_index]
        blocks = jnp.einsum("ksab,kcb->ksac", left_wide, partner_slot, precision=lax.Precision.HIGHEST)
        target = left_rows * RG + right_slot_rows[:, None]
        target = jnp.where(left_valid & (right_slot_rows >= 0)[:, None], target, -1)
        select = (target.reshape(1, slot_total) == positions[:, None]).astype(jnp.float32)
        gained = jnp.dot(select, blocks.reshape(slot_total, -1), precision=lax.Precision.HIGHEST)
        partial_value = partial_value + gained.reshape(partial_value.shape)
    return partial_value


def reference(x_vals, x_rows, out_block):
    listed = out_block.reshape(N_ROW * N_COL, OG)

    def one_tile(tile_index):
        row_group = tile_index // N_COL
        offset = tile_index % N_COL
        partner_group = (row_group + offset - N_COL // 2) % N_ROW
        left_vals = lax.dynamic_index_in_dim(x_vals, row_group, 0, keepdims=False)
        left_rows = lax.dynamic_index_in_dim(x_rows, row_group, 0, keepdims=False)
        right_vals = lax.dynamic_index_in_dim(x_vals, partner_group, 0, keepdims=False)
        right_rows = lax.dynamic_index_in_dim(x_rows, partner_group, 0, keepdims=False)
        positions = lax.dynamic_index_in_dim(listed, tile_index, 0, keepdims=False)
        return tile_sum(left_vals, left_rows, right_vals, right_rows, positions).astype(jnp.bfloat16)

    result = lax.map(one_tile, jnp.arange(N_ROW * N_COL, dtype=jnp.int32))
    return result.reshape(N_ROW, N_COL, OG, BS, BS)
```

```python
import functools

import jax
import jax.numpy as jnp
from jax import lax
from jax.experimental import pallas as pl
from jax.experimental.pallas import tpu as pltpu
from jax.sharding import PartitionSpec as P

MESH = pl.DeviceIdType.MESH


def product(left, right):
    return lax.dot_general(
        left, right, (((1,), (1,)), ((), ())), preferred_element_type=jnp.float32
    )


def kernel(
    sizes, rows_ref, pos_ref, x_ref, out_ref,
    raw, home, partner, pos_vmem, pos_smem, send_parts, recv_parts,
    local_sem, home_send, home_recv, partner_send, partner_recv,
    pos_send, pos_recv, sum_send, sum_recv,
):
    row_count, col_count, depth_count = sizes
    width, slots, size = x_ref.shape[1], x_ref.shape[2], x_ref.shape[3]
    group_rows = home.shape[1]
    midpoint = col_count // 2
    row, col, depth = (lax.axis_index(name) for name in ("row", "col", "depth"))
    has_partner = col != midpoint

    def place(row_index, col_index, depth_index):
        return {"row": row_index, "col": col_index, "depth": depth_index}

    load = pltpu.make_async_copy(x_ref.at[0], raw, local_sem.at[0])
    load.start()

    barrier = pltpu.get_barrier_semaphore()

    def greet(device):
        pl.semaphore_signal(barrier, inc=1, device_id=device, device_id_type=MESH)

    for step in range(1, col_count):
        greet(place(row, lax.rem(col + step, col_count), depth))
    for step in range(1, depth_count):
        greet(place(row, col, lax.rem(depth + step, depth_count)))

    @pl.when(has_partner)
    def _():
        source_row = lax.rem(row + col - midpoint + row_count, row_count)
        for step in range(col_count):
            greet(place(source_row, lax.rem(col + step, col_count), depth))

    pos_vmem[0] = jnp.full(pos_vmem.shape[1:], pos_ref[0, 0, 0], jnp.int32)
    load.wait()
    for column in range(width):
        for block_row in range(group_rows):
            slot = jnp.int32(0)
            found = jnp.int32(0)
            for index in range(slots):
                match = rows_ref[0, column, index] == block_row
                slot = jnp.where(match, index, slot)
                found = jnp.where(match, 1, found)
            block = raw[column, slot]
            home[0, block_row, :, column * size:(column + 1) * size] = jnp.where(
                found > 0, block, jnp.zeros_like(block)
            )

    pl.semaphore_wait(barrier, 2 * (col_count - 1) + depth_count - 1)

    def home_copy(step):
        return pltpu.make_async_remote_copy(
            src_ref=home.at[0],
            dst_ref=home.at[step],
            send_sem=home_send.at[step],
            recv_sem=home_recv.at[step],
            device_id=place(row, lax.rem(col + step, col_count), depth),
            device_id_type=MESH,
        )

    def partner_copy(step):
        target_col = lax.rem(col + step, col_count)
        target_row = lax.rem(row + midpoint - target_col + row_count, row_count)
        return pltpu.make_async_remote_copy(
            src_ref=home.at[0],
            dst_ref=partner.at[step],
            send_sem=partner_send.at[step],
            recv_sem=partner_recv.at[step],
            device_id=place(target_row, target_col, depth),
            device_id_type=MESH,
        )

    def pos_copy(step):
        return pltpu.make_async_remote_copy(
            src_ref=pos_vmem.at[0],
            dst_ref=pos_vmem.at[step],
            send_sem=pos_send.at[step],
            recv_sem=pos_recv.at[step],
            device_id=place(row, col, lax.rem(depth + step, depth_count)),
            device_id_type=MESH,
        )

    def sum_copy(step):
        return pltpu.make_async_remote_copy(
            src_ref=send_parts.at[step],
            dst_ref=recv_parts.at[step],
            send_sem=sum_send.at[step],
            recv_sem=sum_recv.at[step],
            device_id=place(row, col, lax.rem(depth + step, depth_count)),
            device_id_type=MESH,
        )

    def sends_partner(step):
        return lax.rem(col + step, col_count) != midpoint

    for step in range(col_count):
        pl.when(sends_partner(step))(lambda: partner_copy(step).start())
        if step:
            home_copy(step).start()
    for step in range(1, depth_count):
        pos_copy(step).start()

    for step in range(1, depth_count):
        pos_copy(step).wait_recv()
    listed = pltpu.make_async_copy(pos_vmem, pos_smem, local_sem.at[1])
    listed.start()
    listed.wait()
    for step in range(1, col_count):
        home_copy(step).wait_recv()

    def one_entry(right, step):
        position = pos_smem[(depth_count - step) % depth_count, 0, 0]
        left_row = lax.div(position, group_rows)
        right_row = lax.rem(position, group_rows)
        total = product(home[0, left_row], right[0, right_row])
        for index in range(1, col_count):
            total = total + product(home[index, left_row], right[index, right_row])
        return total

    def tile(right):
        for step in range(1, depth_count):
            send_parts[step] = one_entry(right, step)
            sum_copy(step).start()
        send_parts[0] = one_entry(right, 0)

    @pl.when(has_partner)
    def _():
        for step in range(col_count):
            partner_copy(step).wait_recv()
        tile(partner)

    @pl.when(jnp.logical_not(has_partner))
    def _():
        tile(home)

    total = send_parts[0]
    for step in range(1, depth_count):
        sum_copy(step).wait_recv()
        total = total + recv_parts[step]
    out_ref[0, 0, 0] = total.astype(out_ref.dtype)

    for step in range(col_count):
        pl.when(sends_partner(step))(lambda: partner_copy(step).wait_send())
        if step:
            home_copy(step).wait_send()
    for step in range(1, depth_count):
        pos_copy(step).wait_send()
        sum_copy(step).wait_send()


def on_device(sizes, x_vals, x_rows, out_block):
    row_count, col_count, depth_count = sizes
    _, width, slots, size, _ = x_vals.shape
    group_rows = width * col_count * depth_count // row_count
    dma = pltpu.SemaphoreType.DMA
    return pl.pallas_call(
        functools.partial(kernel, sizes),
        out_shape=jax.ShapeDtypeStruct(out_block.shape + (size, size), jnp.bfloat16),
        in_specs=[
            pl.BlockSpec(memory_space=pltpu.SMEM),
            pl.BlockSpec(memory_space=pltpu.SMEM),
            pl.BlockSpec(memory_space=pl.ANY),
        ],
        out_specs=pl.BlockSpec(memory_space=pltpu.VMEM),
        scratch_shapes=[
            pltpu.VMEM((width, slots, size, size), x_vals.dtype),
            pltpu.VMEM((col_count, group_rows, size, width * size), x_vals.dtype),
            pltpu.VMEM((col_count, group_rows, size, width * size), x_vals.dtype),
            pltpu.VMEM((depth_count, 8, 128), jnp.int32),
            pltpu.SMEM((depth_count, 8, 128), jnp.int32),
            pltpu.VMEM((depth_count, size, size), jnp.float32),
            pltpu.VMEM((depth_count, size, size), jnp.float32),
            dma((2,)),
            dma((col_count,)),
            dma((col_count,)),
            dma((col_count,)),
            dma((col_count,)),
            dma((depth_count,)),
            dma((depth_count,)),
            dma((depth_count,)),
            dma((depth_count,)),
        ],
        compiler_params=pltpu.CompilerParams(collective_id=0, has_side_effects=True),
    )(x_rows, out_block, x_vals)


def solution(mesh):
    sizes = tuple(mesh.shape[name] for name in ("row", "col", "depth"))
    in_specs = (
        P("row", ("col", "depth"), None, None, None),
        P("row", ("col", "depth"), None),
        P("row", "col", "depth"),
    )
    out_specs = P("row", "col", "depth", None, None)
    return jax.shard_map(
        functools.partial(on_device, sizes),
        mesh=mesh, in_specs=in_specs, out_specs=out_specs, check_vma=False,
    )
```

```python
import functools

import jax
import jax.numpy as jnp
from jax import lax
from jax.experimental import pallas as pl
from jax.experimental.pallas import tpu as pltpu
from jax.sharding import PartitionSpec as P

MESH = pl.DeviceIdType.MESH
CHUNKS = 4


def product(left, right):
    return lax.dot_general(
        left, right, (((1,), (1,)), ((), ())), preferred_element_type=jnp.float32
    )


def kernel(
    sizes, rows_ref, pos_ref, x_ref, out_ref,
    raw, home, partner, pos_vmem, pos_smem, send_parts, recv_parts,
    local_sem, home_send, home_recv, partner_send, partner_recv,
    pos_send, pos_recv, sum_send, sum_recv,
):
    row_count, col_count, depth_count = sizes
    width, slots, size = x_ref.shape[1], x_ref.shape[2], x_ref.shape[3]
    chunks, group_rows, sub = home.shape[1:4]
    wide = home.shape[4]
    midpoint = col_count // 2
    row, col, depth = (lax.axis_index(name) for name in ("row", "col", "depth"))
    has_partner = col != midpoint

    def place(row_index, col_index, depth_index):
        return {"row": row_index, "col": col_index, "depth": depth_index}

    load = pltpu.make_async_copy(x_ref.at[0], raw, local_sem.at[0])
    load.start()

    barrier = pltpu.get_barrier_semaphore()

    def greet(device):
        pl.semaphore_signal(barrier, inc=1, device_id=device, device_id_type=MESH)

    for step in range(1, col_count):
        greet(place(row, lax.rem(col + step, col_count), depth))
    for step in range(1, depth_count):
        greet(place(row, col, lax.rem(depth + step, depth_count)))

    @pl.when(has_partner)
    def _():
        source_row = lax.rem(row + col - midpoint + row_count, row_count)
        for step in range(col_count):
            greet(place(source_row, lax.rem(col + step, col_count), depth))

    pos_vmem[0] = jnp.full(pos_vmem.shape[1:], pos_ref[0, 0, 0], jnp.int32)
    load.wait()
    for column in range(width):
        for block_row in range(group_rows):
            slot = jnp.int32(0)
            found = jnp.int32(0)
            for index in range(slots):
                match = rows_ref[0, column, index] == block_row
                slot = jnp.where(match, index, slot)
                found = jnp.where(match, 1, found)
            block = raw[column, slot]
            block = jnp.where(found > 0, block, jnp.zeros_like(block))
            home[0, :, block_row, :, column * size:(column + 1) * size] = block.reshape(
                chunks, sub, size
            )

    pl.semaphore_wait(barrier, 2 * (col_count - 1) + depth_count - 1)

    def home_copy(step):
        return pltpu.make_async_remote_copy(
            src_ref=home.at[0],
            dst_ref=home.at[step],
            send_sem=home_send.at[step],
            recv_sem=home_recv.at[step],
            device_id=place(row, lax.rem(col + step, col_count), depth),
            device_id_type=MESH,
        )

    def partner_copy(step, chunk):
        target_col = lax.rem(col + step, col_count)
        target_row = lax.rem(row + midpoint - target_col + row_count, row_count)
        return pltpu.make_async_remote_copy(
            src_ref=home.at[0, chunk],
            dst_ref=partner[chunk].at[step],
            send_sem=partner_send.at[step, chunk],
            recv_sem=partner_recv.at[step, chunk],
            device_id=place(target_row, target_col, depth),
            device_id_type=MESH,
        )

    def pos_copy(step):
        return pltpu.make_async_remote_copy(
            src_ref=pos_vmem.at[0],
            dst_ref=pos_vmem.at[step],
            send_sem=pos_send.at[step],
            recv_sem=pos_recv.at[step],
            device_id=place(row, col, lax.rem(depth + step, depth_count)),
            device_id_type=MESH,
        )

    def sum_copy(step, chunk):
        columns = pl.ds(chunk * sub, sub)
        return pltpu.make_async_remote_copy(
            src_ref=send_parts.at[step, columns],
            dst_ref=recv_parts.at[step, columns],
            send_sem=sum_send.at[step, chunk],
            recv_sem=sum_recv.at[step, chunk],
            device_id=place(row, col, lax.rem(depth + step, depth_count)),
            device_id_type=MESH,
        )

    def sends_partner(step):
        return lax.rem(col + step, col_count) != midpoint

    for chunk in range(chunks):
        for step in range(col_count):
            pl.when(sends_partner(step))(lambda: partner_copy(step, chunk).start())
            if step and not chunk:
                home_copy(step).start()
    for step in range(1, depth_count):
        pos_copy(step).start()

    for step in range(1, depth_count):
        pos_copy(step).wait_recv()
    listed = pltpu.make_async_copy(pos_vmem, pos_smem, local_sem.at[1])
    listed.start()
    listed.wait()
    for step in range(1, col_count):
        home_copy(step).wait_recv()

    def chunk_of_entry(right, step, chunk):
        position = pos_smem[(depth_count - step) % depth_count, 0, 0]
        left_row = lax.div(position, group_rows)
        right_row = lax.rem(position, group_rows)
        total = jnp.zeros((sub, size), jnp.float32)
        for index in range(col_count):
            left = home[index, :, left_row].reshape(size, wide)
            total = total + product(right(index, chunk, right_row), left)
        return total

    def tile(right, chunk):
        columns = slice(chunk * sub, (chunk + 1) * sub)
        for step in range(1, depth_count):
            send_parts[step, columns] = chunk_of_entry(right, step, chunk)
            sum_copy(step, chunk).start()
        send_parts[0, columns] = chunk_of_entry(right, 0, chunk)

    @pl.when(has_partner)
    def _():
        for chunk in range(chunks):
            for step in range(col_count):
                partner_copy(step, chunk).wait_recv()
            tile(lambda index, part, block_row: partner[part][index, block_row], chunk)

    @pl.when(jnp.logical_not(has_partner))
    def _():
        for chunk in range(chunks):
            tile(lambda index, part, block_row: home[index, part, block_row], chunk)

    for chunk in range(chunks):
        columns = slice(chunk * sub, (chunk + 1) * sub)
        total = send_parts[0, columns]
        for step in range(1, depth_count):
            sum_copy(step, chunk).wait_recv()
            total = total + recv_parts[step, columns]
        send_parts[0, columns] = total
    out_ref[0, 0, 0] = send_parts[0].T.astype(out_ref.dtype)

    for step in range(1, col_count):
        home_copy(step).wait_send()
    for step in range(1, depth_count):
        pos_copy(step).wait_send()
    for chunk in range(chunks):
        for step in range(col_count):
            pl.when(sends_partner(step))(lambda: partner_copy(step, chunk).wait_send())
        for step in range(1, depth_count):
            sum_copy(step, chunk).wait_send()


def on_device(sizes, x_vals, x_rows, out_block):
    row_count, col_count, depth_count = sizes
    _, width, slots, size, _ = x_vals.shape
    group_rows = width * col_count * depth_count // row_count
    staged = (col_count, CHUNKS, group_rows, size // CHUNKS, width * size)
    dma = pltpu.SemaphoreType.DMA
    return pl.pallas_call(
        functools.partial(kernel, sizes),
        out_shape=jax.ShapeDtypeStruct(out_block.shape + (size, size), jnp.bfloat16),
        in_specs=[
            pl.BlockSpec(memory_space=pltpu.SMEM),
            pl.BlockSpec(memory_space=pltpu.SMEM),
            pl.BlockSpec(memory_space=pl.ANY),
        ],
        out_specs=pl.BlockSpec(memory_space=pltpu.VMEM),
        scratch_shapes=[
            pltpu.VMEM((width, slots, size, size), x_vals.dtype),
            pltpu.VMEM(staged, x_vals.dtype),
            tuple(pltpu.VMEM(staged[:1] + staged[2:], x_vals.dtype) for _ in range(CHUNKS)),
            pltpu.VMEM((depth_count, 8, 128), jnp.int32),
            pltpu.SMEM((depth_count, 8, 128), jnp.int32),
            pltpu.VMEM((depth_count, size, size), jnp.float32),
            pltpu.VMEM((depth_count, size, size), jnp.float32),
            dma((2,)),
            dma((col_count,)),
            dma((col_count,)),
            dma((col_count, CHUNKS)),
            dma((col_count, CHUNKS)),
            dma((depth_count,)),
            dma((depth_count,)),
            dma((depth_count, CHUNKS)),
            dma((depth_count, CHUNKS)),
        ],
        compiler_params=pltpu.CompilerParams(collective_id=0, has_side_effects=True),
    )(x_rows, out_block, x_vals)


def solution(mesh):
    sizes = tuple(mesh.shape[name] for name in ("row", "col", "depth"))
    in_specs = (
        P("row", ("col", "depth"), None, None, None),
        P("row", ("col", "depth"), None),
        P("row", "col", "depth"),
    )
    out_specs = P("row", "col", "depth", None, None)
    return jax.shard_map(
        functools.partial(on_device, sizes),
        mesh=mesh, in_specs=in_specs, out_specs=out_specs, check_vma=False,
    )
```

```python
import functools

import jax
import jax.numpy as jnp
from jax import lax
from jax.experimental import pallas as pl
from jax.experimental.pallas import tpu as pltpu
from jax.sharding import PartitionSpec as P

MESH = pl.DeviceIdType.MESH
CHUNKS = 4
VMEM_LIMIT = 64 * 1024 * 1024


def product(left, right):
    return lax.dot_general(
        left, right, (((1,), (1,)), ((), ())), preferred_element_type=jnp.float32
    )


def kernel(
    sizes, rows_hbm, pos_ref, x_ref, out_ref,
    rows_ref, raw, home, partner, pos_vmem, send_parts, recv_parts,
    local_sem, home_send, home_recv, partner_send, partner_recv,
    pos_send, pos_recv, sum_send, sum_recv,
):
    row_count, col_count, depth_count = sizes
    width, slots, size = x_ref.shape[1], x_ref.shape[2], x_ref.shape[3]
    chunks, group_rows, sub = home.shape[1:4]
    wide = home.shape[4]
    midpoint = col_count // 2
    row, col, depth = (lax.axis_index(name) for name in ("row", "col", "depth"))
    has_partner = col != midpoint

    def place(row_index, col_index, depth_index):
        return {"row": row_index, "col": col_index, "depth": depth_index}

    loads = [
        pltpu.make_async_copy(x_ref.at[0], raw, local_sem.at[0]),
        pltpu.make_async_copy(rows_hbm, rows_ref, local_sem.at[1]),
        pltpu.make_async_copy(pos_ref.at[0], pos_vmem.at[0], local_sem.at[2]),
    ]
    for copy in loads:
        copy.start()

    barrier = pltpu.get_barrier_semaphore()

    def greet(device):
        pl.semaphore_signal(barrier, inc=1, device_id=device, device_id_type=MESH)

    for step in range(1, col_count):
        greet(place(row, lax.rem(col + step, col_count), depth))
    for step in range(1, depth_count):
        greet(place(row, col, lax.rem(depth + step, depth_count)))

    @pl.when(has_partner)
    def _():
        source_row = lax.rem(row + col - midpoint + row_count, row_count)
        for step in range(col_count):
            greet(place(source_row, lax.rem(col + step, col_count), depth))

    for copy in loads:
        copy.wait()
    for column in range(width):
        for block_row in range(group_rows):
            slot = jnp.int32(0)
            found = jnp.int32(0)
            for index in range(slots):
                match = rows_ref[0, column, index] == block_row
                slot = jnp.where(match, index, slot)
                found = jnp.where(match, 1, found)
            block = raw[column, slot]
            block = jnp.where(found > 0, block, jnp.zeros_like(block))
            home[0, :, block_row, :, column * size:(column + 1) * size] = block.reshape(
                chunks, sub, size
            )

    pl.semaphore_wait(barrier, 2 * (col_count - 1) + depth_count - 1)

    def home_copy(step):
        return pltpu.make_async_remote_copy(
            src_ref=home.at[0],
            dst_ref=home.at[step],
            send_sem=home_send.at[step],
            recv_sem=home_recv.at[step],
            device_id=place(row, lax.rem(col + step, col_count), depth),
            device_id_type=MESH,
        )

    def partner_copy(step, chunk):
        target_col = lax.rem(col + step, col_count)
        target_row = lax.rem(row + midpoint - target_col + row_count, row_count)
        return pltpu.make_async_remote_copy(
            src_ref=home.at[0, chunk],
            dst_ref=partner[chunk].at[step],
            send_sem=partner_send.at[step, chunk],
            recv_sem=partner_recv.at[step, chunk],
            device_id=place(target_row, target_col, depth),
            device_id_type=MESH,
        )

    def pos_copy(step):
        return pltpu.make_async_remote_copy(
            src_ref=pos_vmem.at[0],
            dst_ref=pos_vmem.at[step],
            send_sem=pos_send.at[step],
            recv_sem=pos_recv.at[step],
            device_id=place(row, col, lax.rem(depth + step, depth_count)),
            device_id_type=MESH,
        )

    def sum_copy(step, chunk):
        columns = pl.ds(chunk * sub, sub)
        return pltpu.make_async_remote_copy(
            src_ref=send_parts.at[step, columns],
            dst_ref=recv_parts.at[step, columns],
            send_sem=sum_send.at[step, chunk],
            recv_sem=sum_recv.at[step, chunk],
            device_id=place(row, col, lax.rem(depth + step, depth_count)),
            device_id_type=MESH,
        )

    def sends_partner(step):
        return lax.rem(col + step, col_count) != midpoint

    for step in range(1, depth_count):
        pos_copy(step).start()
    for chunk in range(chunks):
        for step in range(col_count):
            pl.when(sends_partner(step))(lambda: partner_copy(step, chunk).start())
            if step and not chunk:
                home_copy(step).start()
    for step in range(1, depth_count):
        pos_copy(step).wait_recv()
    positions = [pos_vmem[step, 0, 0] for step in range(depth_count)]
    for step in range(1, col_count):
        home_copy(step).wait_recv()

    def chunk_of_entry(right, step, chunk):
        position = positions[(depth_count - step) % depth_count]
        left_row = lax.div(position, group_rows)
        right_row = lax.rem(position, group_rows)
        total = jnp.zeros((sub, size), jnp.float32)
        for index in range(col_count):
            left = home[index, :, left_row].reshape(size, wide)
            total = total + product(right(index, chunk, right_row), left)
        return total

    def tile(right, chunk):
        columns = slice(chunk * sub, (chunk + 1) * sub)
        for step in range(1, depth_count):
            send_parts[step, columns] = chunk_of_entry(right, step, chunk)
            sum_copy(step, chunk).start()
        send_parts[0, columns] = chunk_of_entry(right, 0, chunk)

    @pl.when(has_partner)
    def _():
        for chunk in range(chunks):
            for step in range(col_count):
                partner_copy(step, chunk).wait_recv()
            tile(lambda index, part, block_row: partner[part][index, block_row], chunk)

    @pl.when(jnp.logical_not(has_partner))
    def _():
        for chunk in range(chunks):
            tile(lambda index, part, block_row: home[index, part, block_row], chunk)

    for chunk in range(chunks):
        columns = slice(chunk * sub, (chunk + 1) * sub)
        total = send_parts[0, columns]
        for step in range(1, depth_count):
            sum_copy(step, chunk).wait_recv()
            total = total + recv_parts[step, columns]
        send_parts[0, columns] = total
    out_ref[0, 0, 0] = send_parts[0].T.astype(out_ref.dtype)

    for step in range(1, col_count):
        home_copy(step).wait_send()
    for step in range(1, depth_count):
        pos_copy(step).wait_send()
    for chunk in range(chunks):
        for step in range(col_count):
            pl.when(sends_partner(step))(lambda: partner_copy(step, chunk).wait_send())
        for step in range(1, depth_count):
            sum_copy(step, chunk).wait_send()


def on_device(sizes, x_vals, x_rows, out_block):
    row_count, col_count, depth_count = sizes
    _, width, slots, size, _ = x_vals.shape
    group_rows = width * col_count * depth_count // row_count
    staged = (col_count, CHUNKS, group_rows, size // CHUNKS, width * size)
    dma = pltpu.SemaphoreType.DMA
    return pl.pallas_call(
        functools.partial(kernel, sizes),
        out_shape=jax.ShapeDtypeStruct(out_block.shape + (size, size), jnp.bfloat16),
        in_specs=[
            pl.BlockSpec(memory_space=pl.ANY),
            pl.BlockSpec(memory_space=pl.ANY),
            pl.BlockSpec(memory_space=pl.ANY),
        ],
        out_specs=pl.BlockSpec(memory_space=pltpu.VMEM),
        scratch_shapes=[
            pltpu.SMEM(x_rows.shape, jnp.int32),
            pltpu.VMEM((width, slots, size, size), x_vals.dtype),
            pltpu.VMEM(staged, x_vals.dtype),
            tuple(pltpu.VMEM(staged[:1] + staged[2:], x_vals.dtype) for _ in range(CHUNKS)),
            pltpu.VMEM((depth_count,) + out_block.shape[1:], jnp.int32),
            pltpu.VMEM((depth_count, size, size), jnp.float32),
            pltpu.VMEM((depth_count, size, size), jnp.float32),
            dma((3,)),
            dma((col_count,)),
            dma((col_count,)),
            dma((col_count, CHUNKS)),
            dma((col_count, CHUNKS)),
            dma((depth_count,)),
            dma((depth_count,)),
            dma((depth_count, CHUNKS)),
            dma((depth_count, CHUNKS)),
        ],
        compiler_params=pltpu.CompilerParams(
            collective_id=0, has_side_effects=True, vmem_limit_bytes=VMEM_LIMIT
        ),
    )(x_rows, out_block, x_vals)


def solution(mesh):
    sizes = tuple(mesh.shape[name] for name in ("row", "col", "depth"))
    in_specs = (
        P("row", ("col", "depth"), None, None, None),
        P("row", ("col", "depth"), None),
        P("row", "col", "depth"),
    )
    out_specs = P("row", "col", "depth", None, None)
    return jax.shard_map(
        functools.partial(on_device, sizes),
        mesh=mesh, in_specs=in_specs, out_specs=out_specs, check_vma=False,
    )
```

```python
import functools

import jax
import jax.numpy as jnp
from jax import lax
from jax.experimental import pallas as pl
from jax.experimental.pallas import tpu as pltpu
from jax.sharding import PartitionSpec as P

MESH = pl.DeviceIdType.MESH
CHUNKS = 4
VMEM_LIMIT = 64 * 1024 * 1024


def product(left, right):
    return lax.dot_general(
        left, right, (((1,), (1,)), ((), ())), preferred_element_type=jnp.float32
    )


def kernel(
    sizes, rows_hbm, pos_ref, x_ref, out_ref,
    home, home_rows, partner, partner_rows, rows_smem, pos_vmem,
    left, send_parts, recv_parts,
    local_sem, home_send, home_recv, partner_send, partner_recv,
    row_send, row_recv, pos_send, pos_recv, sum_send, sum_recv,
):
    row_count, col_count, depth_count = sizes
    width, slots, size = x_ref.shape[1], x_ref.shape[2], x_ref.shape[3]
    chunks, sub = len(partner), partner[0].shape[3]
    group_rows = width * col_count * depth_count // row_count
    midpoint = col_count // 2
    row, col, depth = (lax.axis_index(name) for name in ("row", "col", "depth"))
    has_partner = col != midpoint

    def place(row_index, col_index, depth_index):
        return {"row": row_index, "col": col_index, "depth": depth_index}

    loads = [
        pltpu.make_async_copy(x_ref.at[0], home.at[0], local_sem.at[0]),
        pltpu.make_async_copy(rows_hbm.at[0], home_rows.at[0], local_sem.at[1]),
        pltpu.make_async_copy(pos_ref.at[0], pos_vmem.at[0], local_sem.at[2]),
    ]
    for copy in loads:
        copy.start()

    barrier = pltpu.get_barrier_semaphore()

    def greet(device):
        pl.semaphore_signal(barrier, inc=1, device_id=device, device_id_type=MESH)

    for step in range(1, col_count):
        greet(place(row, lax.rem(col + step, col_count), depth))
    for step in range(1, depth_count):
        greet(place(row, col, lax.rem(depth + step, depth_count)))

    @pl.when(has_partner)
    def _():
        source_row = lax.rem(row + col - midpoint + row_count, row_count)
        for step in range(col_count):
            greet(place(source_row, lax.rem(col + step, col_count), depth))

    pl.semaphore_wait(barrier, 2 * (col_count - 1) + depth_count - 1)

    def home_device(step):
        return place(row, lax.rem(col + step, col_count), depth)

    def partner_device(step):
        target_col = lax.rem(col + step, col_count)
        target_row = lax.rem(row + midpoint - target_col + row_count, row_count)
        return place(target_row, target_col, depth)

    def depth_device(step):
        return place(row, col, lax.rem(depth + step, depth_count))

    def send(source, target, send_sem, recv_sem, device):
        return pltpu.make_async_remote_copy(
            src_ref=source, dst_ref=target, send_sem=send_sem, recv_sem=recv_sem,
            device_id=device, device_id_type=MESH,
        )

    def home_copy(step):
        return send(
            x_ref.at[0], home.at[step],
            home_send.at[step], home_recv.at[step], home_device(step),
        )

    def home_rows_copy(step):
        return send(
            rows_hbm.at[0], home_rows.at[step],
            row_send.at[0, step], row_recv.at[0, step], home_device(step),
        )

    def partner_copy(step, chunk):
        return send(
            x_ref.at[0, :, :, pl.ds(chunk * sub, sub)], partner[chunk].at[step],
            partner_send.at[step, chunk], partner_recv.at[step, chunk],
            partner_device(step),
        )

    def partner_rows_copy(step):
        return send(
            rows_hbm.at[0], partner_rows.at[step],
            row_send.at[1, step], row_recv.at[1, step], partner_device(step),
        )

    def pos_copy(step):
        return send(
            pos_vmem.at[0], pos_vmem.at[step],
            pos_send.at[step], pos_recv.at[step], depth_device(step),
        )

    def sum_copy(step, chunk):
        columns = pl.ds(chunk * sub, sub)
        return send(
            send_parts.at[step, columns], recv_parts.at[step, columns],
            sum_send.at[step, chunk], sum_recv.at[step, chunk], depth_device(step),
        )

    def sends_partner(step):
        return lax.rem(col + step, col_count) != midpoint

    for step in range(col_count):
        pl.when(sends_partner(step))(lambda: partner_copy(step, 0).start())
    loads[2].wait()
    for step in range(1, depth_count):
        pos_copy(step).start()
    for step in range(col_count):
        if step:
            home_rows_copy(step).start()
            home_copy(step).start()
        pl.when(sends_partner(step))(lambda: partner_rows_copy(step).start())
    for chunk in range(1, chunks):
        for step in range(col_count):
            pl.when(sends_partner(step))(lambda: partner_copy(step, chunk).start())

    for copy in loads[:2]:
        copy.wait()
    for step in range(1, col_count):
        home_rows_copy(step).wait_recv()
    to_smem = pltpu.make_async_copy(home_rows, rows_smem.at[0], local_sem.at[3])
    to_smem.start()
    for step in range(1, depth_count):
        pos_copy(step).wait_recv()
    positions = [
        pos_vmem[(depth_count - step) % depth_count, 0, 0] for step in range(depth_count)
    ]
    to_smem.wait()
    for step in range(1, col_count):
        home_copy(step).wait_recv()

    def pick(side, read, index, block_row):
        found_blocks = []
        for column in range(width):
            slot = jnp.int32(0)
            found = jnp.int32(0)
            for number in range(slots):
                match = rows_smem[side, index, column, number] == block_row
                slot = jnp.where(match, number, slot)
                found = jnp.where(match, 1, found)
            block = read(index, column, slot)
            found_blocks.append(jnp.where(found > 0, block, jnp.zeros_like(block)))
        return jnp.concatenate(found_blocks, axis=1)

    steps = list(range(1, depth_count)) + [0]
    for step in steps:
        for index in range(col_count):
            left[step, index] = pick(
                0, lambda at, column, slot: home[at, column, slot],
                index, lax.div(positions[step], group_rows),
            )

    def tile(side, read, chunk):
        columns = slice(chunk * sub, (chunk + 1) * sub)
        for step in steps:
            right_row = lax.rem(positions[step], group_rows)
            total = jnp.zeros((sub, size), jnp.float32)
            for index in range(col_count):
                total = total + product(pick(side, read, index, right_row), left[step, index])
            send_parts[step, columns] = total
            if step:
                sum_copy(step, chunk).start()

    @pl.when(has_partner)
    def _():
        for step in range(col_count):
            partner_rows_copy(step).wait_recv()
        moved = pltpu.make_async_copy(partner_rows, rows_smem.at[1], local_sem.at[4])
        moved.start()
        moved.wait()
        for chunk in range(chunks):
            for step in range(col_count):
                partner_copy(step, chunk).wait_recv()
            tile(1, lambda at, column, slot: partner[chunk][at, column, slot], chunk)

    @pl.when(jnp.logical_not(has_partner))
    def _():
        for chunk in range(chunks):
            columns = slice(chunk * sub, (chunk + 1) * sub)
            tile(0, lambda at, column, slot: home[at, column, slot, columns], chunk)

    for chunk in range(chunks):
        columns = slice(chunk * sub, (chunk + 1) * sub)
        total = send_parts[0, columns]
        for step in range(1, depth_count):
            sum_copy(step, chunk).wait_recv()
            total = total + recv_parts[step, columns]
        send_parts[0, columns] = total
    out_ref[0, 0, 0] = send_parts[0].T.astype(out_ref.dtype)

    for step in range(col_count):
        if step:
            home_copy(step).wait_send()
            home_rows_copy(step).wait_send()
        pl.when(sends_partner(step))(lambda: partner_rows_copy(step).wait_send())
    for step in range(1, depth_count):
        pos_copy(step).wait_send()
    for chunk in range(chunks):
        for step in range(col_count):
            pl.when(sends_partner(step))(lambda: partner_copy(step, chunk).wait_send())
        for step in range(1, depth_count):
            sum_copy(step, chunk).wait_send()


def on_device(sizes, x_vals, x_rows, out_block):
    row_count, col_count, depth_count = sizes
    _, width, slots, size, _ = x_vals.shape
    sub = size // CHUNKS
    block_set = (col_count, width, slots)
    dma = pltpu.SemaphoreType.DMA
    return pl.pallas_call(
        functools.partial(kernel, sizes),
        out_shape=jax.ShapeDtypeStruct(out_block.shape + (size, size), jnp.bfloat16),
        in_specs=[
            pl.BlockSpec(memory_space=pl.ANY),
            pl.BlockSpec(memory_space=pl.ANY),
            pl.BlockSpec(memory_space=pl.ANY),
        ],
        out_specs=pl.BlockSpec(memory_space=pltpu.VMEM),
        scratch_shapes=[
            pltpu.VMEM(block_set + (size, size), x_vals.dtype),
            pltpu.VMEM(block_set, jnp.int32),
            tuple(pltpu.VMEM(block_set + (sub, size), x_vals.dtype) for _ in range(CHUNKS)),
            pltpu.VMEM(block_set, jnp.int32),
            pltpu.SMEM((2,) + block_set, jnp.int32),
            pltpu.VMEM((depth_count,) + out_block.shape[1:], jnp.int32),
            pltpu.VMEM((depth_count, col_count, size, width * size), x_vals.dtype),
            pltpu.VMEM((depth_count, size, size), jnp.float32),
            pltpu.VMEM((depth_count, size, size), jnp.float32),
            dma((5,)),
            dma((col_count,)),
            dma((col_count,)),
            dma((col_count, CHUNKS)),
            dma((col_count, CHUNKS)),
            dma((2, col_count)),
            dma((2, col_count)),
            dma((depth_count,)),
            dma((depth_count,)),
            dma((depth_count, CHUNKS)),
            dma((depth_count, CHUNKS)),
        ],
        compiler_params=pltpu.CompilerParams(
            collective_id=0, has_side_effects=True, vmem_limit_bytes=VMEM_LIMIT
        ),
    )(x_rows, out_block, x_vals)


def solution(mesh):
    sizes = tuple(mesh.shape[name] for name in ("row", "col", "depth"))
    in_specs = (
        P("row", ("col", "depth"), None, None, None),
        P("row", ("col", "depth"), None),
        P("row", "col", "depth"),
    )
    out_specs = P("row", "col", "depth", None, None)
    return jax.shard_map(
        functools.partial(on_device, sizes),
        mesh=mesh, in_specs=in_specs, out_specs=out_specs, check_vma=False,
    )
```

```python
import functools

import jax
import jax.numpy as jnp
from jax import lax
from jax.experimental import pallas as pl
from jax.experimental.pallas import tpu as pltpu
from jax.sharding import PartitionSpec as P

MESH = pl.DeviceIdType.MESH
CHUNKS = 4
VMEM_LIMIT = 64 * 1024 * 1024


def product(left, right):
    return lax.dot_general(
        left, right, (((1,), (1,)), ((), ())), preferred_element_type=jnp.float32
    )


def kernel(
    sizes, rows_hbm, pos_ref, x_ref, out_ref,
    home, home_rows, partner, partner_rows, rows_smem, pos_vmem,
    left, send_parts, recv_parts,
    local_sem, home_send, home_recv, partner_send, partner_recv,
    row_send, row_recv, pos_send, pos_recv, sum_send, sum_recv,
):
    row_count, col_count, depth_count = sizes
    width, slots, size = x_ref.shape[1], x_ref.shape[2], x_ref.shape[3]
    chunks, sub = len(partner), partner[0].shape[3]
    group_rows = width * col_count * depth_count // row_count
    midpoint = col_count // 2
    row, col, depth = (lax.axis_index(name) for name in ("row", "col", "depth"))
    has_partner = col != midpoint

    def place(row_index, col_index, depth_index):
        return {"row": row_index, "col": col_index, "depth": depth_index}

    loads = [
        pltpu.make_async_copy(x_ref.at[0], home.at[0], local_sem.at[0]),
        pltpu.make_async_copy(rows_hbm.at[0], home_rows.at[0], local_sem.at[1]),
        pltpu.make_async_copy(pos_ref.at[0], pos_vmem.at[0], local_sem.at[2]),
    ]
    for copy in loads:
        copy.start()

    barrier = pltpu.get_barrier_semaphore()

    def greet(device):
        pl.semaphore_signal(barrier, inc=1, device_id=device, device_id_type=MESH)

    for step in range(1, col_count):
        greet(place(row, lax.rem(col + step, col_count), depth))
    for step in range(1, depth_count):
        greet(place(row, col, lax.rem(depth + step, depth_count)))

    @pl.when(has_partner)
    def _():
        source_row = lax.rem(row + col - midpoint + row_count, row_count)
        for step in range(col_count):
            greet(place(source_row, lax.rem(col + step, col_count), depth))

    pl.semaphore_wait(barrier, 2 * (col_count - 1) + depth_count - 1)

    def home_device(step):
        return place(row, lax.rem(col + step, col_count), depth)

    def partner_device(step):
        target_col = lax.rem(col + step, col_count)
        target_row = lax.rem(row + midpoint - target_col + row_count, row_count)
        return place(target_row, target_col, depth)

    def depth_device(step):
        return place(row, col, lax.rem(depth + step, depth_count))

    def send(source, target, send_sem, recv_sem, device):
        return pltpu.make_async_remote_copy(
            src_ref=source, dst_ref=target, send_sem=send_sem, recv_sem=recv_sem,
            device_id=device, device_id_type=MESH,
        )

    def home_copy(step):
        return send(
            x_ref.at[0], home.at[step],
            home_send.at[step], home_recv.at[step], home_device(step),
        )

    def home_rows_copy(step):
        return send(
            rows_hbm.at[0], home_rows.at[step],
            row_send.at[0, step], row_recv.at[0, step], home_device(step),
        )

    def partner_copy(step, chunk):
        return send(
            x_ref.at[0, :, :, pl.ds(chunk * sub, sub)], partner[chunk].at[step],
            partner_send.at[step, chunk], partner_recv.at[step, chunk],
            partner_device(step),
        )

    def partner_rows_copy(step):
        return send(
            rows_hbm.at[0], partner_rows.at[step],
            row_send.at[1, step], row_recv.at[1, step], partner_device(step),
        )

    def pos_copy(step):
        return send(
            pos_vmem.at[0], pos_vmem.at[step],
            pos_send.at[step], pos_recv.at[step], depth_device(step),
        )

    def sum_copy(step, chunk):
        columns = pl.ds(chunk * sub, sub)
        return send(
            send_parts.at[step, columns], recv_parts.at[step, columns],
            sum_send.at[step, chunk], sum_recv.at[step, chunk], depth_device(step),
        )

    def sends_partner(step):
        return lax.rem(col + step, col_count) != midpoint

    for step in range(col_count):
        pl.when(sends_partner(step))(lambda: partner_copy(step, 0).start())
    loads[2].wait()
    for step in range(1, depth_count):
        pos_copy(step).start()
    for step in range(col_count):
        if step:
            home_rows_copy(step).start()
            home_copy(step).start()
        pl.when(sends_partner(step))(lambda: partner_rows_copy(step).start())
    for chunk in range(1, chunks):
        for step in range(col_count):
            pl.when(sends_partner(step))(lambda: partner_copy(step, chunk).start())

    for copy in loads[:2]:
        copy.wait()
    for step in range(1, col_count):
        home_rows_copy(step).wait_recv()
    to_smem = pltpu.make_async_copy(home_rows, rows_smem.at[0], local_sem.at[3])
    to_smem.start()
    for step in range(1, depth_count):
        pos_copy(step).wait_recv()
    positions = [
        pos_vmem[(depth_count - step) % depth_count, 0, 0] for step in range(depth_count)
    ]
    to_smem.wait()
    for step in range(1, col_count):
        home_copy(step).wait_recv()

    def find(side, block_row):
        places = []
        for index in range(col_count):
            for column in range(width):
                slot = jnp.int32(0)
                found = jnp.int32(0)
                for number in range(slots):
                    match = rows_smem[side, index, column, number] == block_row
                    slot = jnp.where(match, number, slot)
                    found = jnp.where(match, 1, found)
                places.append((index, column, slot, found))
        return places

    def pick(places, read):
        blocks = []
        for index, column, slot, found in places:
            block = read(index, column, slot)
            blocks.append(jnp.where(found > 0, block, jnp.zeros_like(block)))
        return jnp.concatenate(blocks, axis=1)

    steps = list(range(1, depth_count)) + [0]
    for step in steps:
        left[step] = pick(
            find(0, lax.div(positions[step], group_rows)),
            lambda index, column, slot: home[index, column, slot],
        )

    def find_all(side):
        return [find(side, lax.rem(positions[step], group_rows)) for step in range(depth_count)]

    def tile(places, read, chunk):
        columns = slice(chunk * sub, (chunk + 1) * sub)
        totals = [product(pick(places[step], read), left[step]) for step in steps]
        for step, total in zip(steps, totals):
            send_parts[step, columns] = total
        for step in range(1, depth_count):
            sum_copy(step, chunk).start()

    @pl.when(has_partner)
    def _():
        for step in range(col_count):
            partner_rows_copy(step).wait_recv()
        moved = pltpu.make_async_copy(partner_rows, rows_smem.at[1], local_sem.at[4])
        moved.start()
        moved.wait()
        places = find_all(1)
        for chunk in range(chunks):
            for step in range(col_count):
                partner_copy(step, chunk).wait_recv()
            tile(places, lambda at, column, slot: partner[chunk][at, column, slot], chunk)

    @pl.when(jnp.logical_not(has_partner))
    def _():
        places = find_all(0)
        for chunk in range(chunks):
            columns = slice(chunk * sub, (chunk + 1) * sub)
            tile(places, lambda at, column, slot: home[at, column, slot, columns], chunk)

    for chunk in range(chunks):
        columns = slice(chunk * sub, (chunk + 1) * sub)
        total = send_parts[0, columns]
        for step in range(1, depth_count):
            sum_copy(step, chunk).wait_recv()
            total = total + recv_parts[step, columns]
        send_parts[0, columns] = total
    out_ref[0, 0, 0] = send_parts[0].T.astype(out_ref.dtype)

    for step in range(col_count):
        if step:
            home_copy(step).wait_send()
            home_rows_copy(step).wait_send()
        pl.when(sends_partner(step))(lambda: partner_rows_copy(step).wait_send())
    for step in range(1, depth_count):
        pos_copy(step).wait_send()
    for chunk in range(chunks):
        for step in range(col_count):
            pl.when(sends_partner(step))(lambda: partner_copy(step, chunk).wait_send())
        for step in range(1, depth_count):
            sum_copy(step, chunk).wait_send()


def on_device(sizes, x_vals, x_rows, out_block):
    row_count, col_count, depth_count = sizes
    _, width, slots, size, _ = x_vals.shape
    sub = size // CHUNKS
    block_set = (col_count, width, slots)
    dma = pltpu.SemaphoreType.DMA
    return pl.pallas_call(
        functools.partial(kernel, sizes),
        out_shape=jax.ShapeDtypeStruct(out_block.shape + (size, size), jnp.bfloat16),
        in_specs=[
            pl.BlockSpec(memory_space=pl.ANY),
            pl.BlockSpec(memory_space=pl.ANY),
            pl.BlockSpec(memory_space=pl.ANY),
        ],
        out_specs=pl.BlockSpec(memory_space=pltpu.VMEM),
        scratch_shapes=[
            pltpu.VMEM(block_set + (size, size), x_vals.dtype),
            pltpu.VMEM(block_set, jnp.int32),
            tuple(pltpu.VMEM(block_set + (sub, size), x_vals.dtype) for _ in range(CHUNKS)),
            pltpu.VMEM(block_set, jnp.int32),
            pltpu.SMEM((2,) + block_set, jnp.int32),
            pltpu.VMEM((depth_count,) + out_block.shape[1:], jnp.int32),
            pltpu.VMEM((depth_count, size, col_count * width * size), x_vals.dtype),
            pltpu.VMEM((depth_count, size, size), jnp.float32),
            pltpu.VMEM((depth_count, size, size), jnp.float32),
            dma((5,)),
            dma((col_count,)),
            dma((col_count,)),
            dma((col_count, CHUNKS)),
            dma((col_count, CHUNKS)),
            dma((2, col_count)),
            dma((2, col_count)),
            dma((depth_count,)),
            dma((depth_count,)),
            dma((depth_count, CHUNKS)),
            dma((depth_count, CHUNKS)),
        ],
        compiler_params=pltpu.CompilerParams(
            collective_id=0, has_side_effects=True, vmem_limit_bytes=VMEM_LIMIT
        ),
    )(x_rows, out_block, x_vals)


def solution(mesh):
    sizes = tuple(mesh.shape[name] for name in ("row", "col", "depth"))
    in_specs = (
        P("row", ("col", "depth"), None, None, None),
        P("row", ("col", "depth"), None),
        P("row", "col", "depth"),
    )
    out_specs = P("row", "col", "depth", None, None)
    return jax.shard_map(
        functools.partial(on_device, sizes),
        mesh=mesh, in_specs=in_specs, out_specs=out_specs, check_vma=False,
    )
```

```python
import functools

import jax
import jax.numpy as jnp
from jax import lax
from jax.experimental import pallas as pl
from jax.experimental.pallas import tpu as pltpu
from jax.sharding import PartitionSpec as P

MESH = pl.DeviceIdType.MESH
CHUNKS = 4
IN_FLIGHT = 2
VMEM_LIMIT = 10 * 1024 * 1024


def product(left, right):
    return lax.dot_general(
        left, right, (((1,), (1,)), ((), ())), preferred_element_type=jnp.float32
    )


def kernel(
    sizes, rows_hbm, pos_ref, x_ref, out_ref,
    home, home_rows, partner, partner_rows, rows_smem, pos_vmem,
    left, send_parts, recv_parts,
    local_sem, home_send, home_recv, partner_send, partner_recv,
    row_send, row_recv, pos_send, pos_recv, sum_send, sum_recv,
):
    row_count, col_count, depth_count = sizes
    width, slots, size = x_ref.shape[1], x_ref.shape[2], x_ref.shape[3]
    chunks, sub = len(partner), partner[0].shape[3]
    group_rows = width * col_count * depth_count // row_count
    midpoint = col_count // 2
    row, col, depth = (lax.axis_index(name) for name in ("row", "col", "depth"))
    has_partner = col != midpoint

    def place(row_index, col_index, depth_index):
        return {"row": row_index, "col": col_index, "depth": depth_index}

    loads = [
        pltpu.make_async_copy(x_ref.at[0], home.at[0], local_sem.at[0]),
        pltpu.make_async_copy(rows_hbm.at[0], home_rows.at[0], local_sem.at[1]),
        pltpu.make_async_copy(pos_ref.at[0], pos_vmem.at[0], local_sem.at[2]),
    ]
    for copy in loads:
        copy.start()

    barrier = pltpu.get_barrier_semaphore()

    def greet(device):
        pl.semaphore_signal(barrier, inc=1, device_id=device, device_id_type=MESH)

    for step in range(1, col_count):
        greet(place(row, lax.rem(col + step, col_count), depth))
    for step in range(1, depth_count):
        greet(place(row, col, lax.rem(depth + step, depth_count)))

    @pl.when(has_partner)
    def _():
        source_row = lax.rem(row + col - midpoint + row_count, row_count)
        for step in range(col_count):
            greet(place(source_row, lax.rem(col + step, col_count), depth))

    pl.semaphore_wait(barrier, 2 * (col_count - 1) + depth_count - 1)

    def home_device(step):
        return place(row, lax.rem(col + step, col_count), depth)

    def partner_device(step):
        target_col = lax.rem(col + step, col_count)
        target_row = lax.rem(row + midpoint - target_col + row_count, row_count)
        return place(target_row, target_col, depth)

    def depth_device(step):
        return place(row, col, lax.rem(depth + step, depth_count))

    def send(source, target, send_sem, recv_sem, device):
        return pltpu.make_async_remote_copy(
            src_ref=source, dst_ref=target, send_sem=send_sem, recv_sem=recv_sem,
            device_id=device, device_id_type=MESH,
        )

    def home_copy(step):
        return send(
            x_ref.at[0], home.at[step],
            home_send.at[step], home_recv.at[step], home_device(step),
        )

    def home_rows_copy(step):
        return send(
            rows_hbm.at[0], home_rows.at[step],
            row_send.at[0, step], row_recv.at[0, step], home_device(step),
        )

    def partner_copy(step, chunk):
        return send(
            x_ref.at[0, :, :, pl.ds(chunk * sub, sub)], partner[chunk].at[step],
            partner_send.at[step, chunk], partner_recv.at[step, chunk],
            partner_device(step),
        )

    def partner_rows_copy(step):
        return send(
            rows_hbm.at[0], partner_rows.at[step],
            row_send.at[1, step], row_recv.at[1, step], partner_device(step),
        )

    def pos_copy(step):
        return send(
            pos_vmem.at[0], pos_vmem.at[step],
            pos_send.at[step], pos_recv.at[step], depth_device(step),
        )

    def sum_copy(step, chunk):
        columns = pl.ds(chunk * sub, sub)
        return send(
            send_parts.at[step, columns], recv_parts.at[step, columns],
            sum_send.at[step, chunk], sum_recv.at[step, chunk], depth_device(step),
        )

    def sends_partner(step):
        return lax.rem(col + step, col_count) != midpoint

    def start_partner(chunk):
        for step in range(col_count):
            if chunk < chunks:
                pl.when(sends_partner(step))(lambda: partner_copy(step, chunk).start())

    def follow_partner(chunk):
        for step in range(col_count):
            pl.when(sends_partner(step))(lambda: partner_copy(step, chunk).wait_send())
        start_partner(chunk + IN_FLIGHT)

    start_partner(0)
    loads[2].wait()
    for step in range(1, depth_count):
        pos_copy(step).start()
    for step in range(col_count):
        if step:
            home_rows_copy(step).start()
            home_copy(step).start()
        pl.when(sends_partner(step))(lambda: partner_rows_copy(step).start())
    for chunk in range(1, IN_FLIGHT):
        start_partner(chunk)

    for copy in loads[:2]:
        copy.wait()
    for step in range(1, col_count):
        home_rows_copy(step).wait_recv()
    to_smem = pltpu.make_async_copy(home_rows, rows_smem.at[0], local_sem.at[3])
    to_smem.start()
    for step in range(1, depth_count):
        pos_copy(step).wait_recv()
    positions = [
        pos_vmem[(depth_count - step) % depth_count, 0, 0] for step in range(depth_count)
    ]
    to_smem.wait()
    for step in range(1, col_count):
        home_copy(step).wait_recv()

    def find(side, block_row):
        places = []
        for index in range(col_count):
            for column in range(width):
                slot = jnp.int32(0)
                found = jnp.int32(0)
                for number in range(slots):
                    match = rows_smem[side, index, column, number] == block_row
                    slot = jnp.where(match, number, slot)
                    found = jnp.where(match, 1, found)
                places.append((index, column, slot, found))
        return places

    def pick(places, read):
        blocks = []
        for index, column, slot, found in places:
            block = read(index, column, slot)
            blocks.append(jnp.where(found > 0, block, jnp.zeros_like(block)))
        return jnp.concatenate(blocks, axis=1)

    steps = list(range(1, depth_count)) + [0]
    for step in steps:
        left[step] = pick(
            find(0, lax.div(positions[step], group_rows)),
            lambda index, column, slot: home[index, column, slot],
        )

    def find_all(side):
        return [find(side, lax.rem(positions[step], group_rows)) for step in range(depth_count)]

    def tile(places, read, chunk):
        columns = slice(chunk * sub, (chunk + 1) * sub)
        totals = [product(pick(places[step], read), left[step]) for step in steps]
        for step, total in zip(steps, totals):
            send_parts[step, columns] = total
        for step in range(1, depth_count):
            sum_copy(step, chunk).start()

    @pl.when(has_partner)
    def _():
        for step in range(col_count):
            partner_rows_copy(step).wait_recv()
        moved = pltpu.make_async_copy(partner_rows, rows_smem.at[1], local_sem.at[4])
        moved.start()
        moved.wait()
        places = find_all(1)
        for chunk in range(chunks):
            follow_partner(chunk)
            for step in range(col_count):
                partner_copy(step, chunk).wait_recv()
            tile(places, lambda at, column, slot: partner[chunk][at, column, slot], chunk)

    @pl.when(jnp.logical_not(has_partner))
    def _():
        places = find_all(0)
        for chunk in range(chunks):
            columns = slice(chunk * sub, (chunk + 1) * sub)
            tile(places, lambda at, column, slot: home[at, column, slot, columns], chunk)
            follow_partner(chunk)

    for chunk in range(chunks):
        columns = slice(chunk * sub, (chunk + 1) * sub)
        total = send_parts[0, columns]
        for step in range(1, depth_count):
            sum_copy(step, chunk).wait_recv()
            total = total + recv_parts[step, columns]
        send_parts[0, columns] = total
    out_ref[0, 0, 0] = send_parts[0].T.astype(out_ref.dtype)

    for step in range(col_count):
        if step:
            home_copy(step).wait_send()
            home_rows_copy(step).wait_send()
        pl.when(sends_partner(step))(lambda: partner_rows_copy(step).wait_send())
    for step in range(1, depth_count):
        pos_copy(step).wait_send()
        for chunk in range(chunks):
            sum_copy(step, chunk).wait_send()


def on_device(sizes, x_vals, x_rows, out_block):
    row_count, col_count, depth_count = sizes
    _, width, slots, size, _ = x_vals.shape
    sub = size // CHUNKS
    block_set = (col_count, width, slots)
    dma = pltpu.SemaphoreType.DMA
    return pl.pallas_call(
        functools.partial(kernel, sizes),
        out_shape=jax.ShapeDtypeStruct(out_block.shape + (size, size), jnp.bfloat16),
        in_specs=[
            pl.BlockSpec(memory_space=pl.ANY),
            pl.BlockSpec(memory_space=pl.ANY),
            pl.BlockSpec(memory_space=pl.ANY),
        ],
        out_specs=pl.BlockSpec(memory_space=pltpu.VMEM),
        scratch_shapes=[
            pltpu.VMEM(block_set + (size, size), x_vals.dtype),
            pltpu.VMEM(block_set, jnp.int32),
            tuple(pltpu.VMEM(block_set + (sub, size), x_vals.dtype) for _ in range(CHUNKS)),
            pltpu.VMEM(block_set, jnp.int32),
            pltpu.SMEM((2,) + block_set, jnp.int32),
            pltpu.VMEM((depth_count,) + out_block.shape[1:], jnp.int32),
            pltpu.VMEM((depth_count, size, col_count * width * size), x_vals.dtype),
            pltpu.VMEM((depth_count, size, size), jnp.float32),
            pltpu.VMEM((depth_count, size, size), jnp.float32),
            dma((5,)),
            dma((col_count,)),
            dma((col_count,)),
            dma((col_count, CHUNKS)),
            dma((col_count, CHUNKS)),
            dma((2, col_count)),
            dma((2, col_count)),
            dma((depth_count,)),
            dma((depth_count,)),
            dma((depth_count, CHUNKS)),
            dma((depth_count, CHUNKS)),
        ],
        compiler_params=pltpu.CompilerParams(
            collective_id=0, has_side_effects=True, vmem_limit_bytes=VMEM_LIMIT
        ),
    )(x_rows, out_block, x_vals)


def solution(mesh):
    sizes = tuple(mesh.shape[name] for name in ("row", "col", "depth"))
    in_specs = (
        P("row", ("col", "depth"), None, None, None),
        P("row", ("col", "depth"), None),
        P("row", "col", "depth"),
    )
    out_specs = P("row", "col", "depth", None, None)
    return jax.shard_map(
        functools.partial(on_device, sizes),
        mesh=mesh, in_specs=in_specs, out_specs=out_specs, check_vma=False,
    )
```

```python
import functools

import jax
import jax.numpy as jnp
from jax import lax
from jax.experimental import pallas as pl
from jax.experimental.pallas import tpu as pltpu
from jax.sharding import PartitionSpec as P

MESH = pl.DeviceIdType.MESH
CHUNKS = 4
VMEM_LIMIT = 55072 * 1024


def product(left, right):
    return lax.dot_general(
        left, right, (((1,), (1,)), ((), ())), preferred_element_type=jnp.float32
    )


def kernel(
    sizes, rows_hbm, pos_ref, x_ref, out_ref,
    home, home_rows, partner, partner_rows, rows_smem, pos_vmem,
    left, send_parts, recv_parts,
    local_sem, home_send, home_recv, partner_send, partner_recv,
    row_send, row_recv, pos_send, pos_recv, sum_send, sum_recv,
):
    row_count, col_count, depth_count = sizes
    width, slots, size = x_ref.shape[1], x_ref.shape[2], x_ref.shape[3]
    chunks, sub = len(partner), partner[0].shape[3]
    group_rows = width * col_count * depth_count // row_count
    midpoint = col_count // 2
    row, col, depth = (lax.axis_index(name) for name in ("row", "col", "depth"))
    has_partner = col != midpoint

    def place(row_index, col_index, depth_index):
        return {"row": row_index, "col": col_index, "depth": depth_index}

    loads = [
        pltpu.make_async_copy(x_ref.at[0], home.at[0], local_sem.at[0]),
        pltpu.make_async_copy(rows_hbm.at[0], home_rows.at[0], local_sem.at[1]),
        pltpu.make_async_copy(pos_ref.at[0], pos_vmem.at[0], local_sem.at[2]),
    ]
    for copy in loads:
        copy.start()

    barrier = pltpu.get_barrier_semaphore()

    def greet(device):
        pl.semaphore_signal(barrier, inc=1, device_id=device, device_id_type=MESH)

    for step in range(1, col_count):
        greet(place(row, lax.rem(col + step, col_count), depth))
    for step in range(1, depth_count):
        greet(place(row, col, lax.rem(depth + step, depth_count)))

    @pl.when(has_partner)
    def _():
        source_row = lax.rem(row + col - midpoint + row_count, row_count)
        for step in range(col_count):
            greet(place(source_row, lax.rem(col + step, col_count), depth))

    pl.semaphore_wait(barrier, 2 * (col_count - 1) + depth_count - 1)

    def home_device(step):
        return place(row, lax.rem(col + step, col_count), depth)

    def partner_device(step):
        target_col = lax.rem(col + step, col_count)
        target_row = lax.rem(row + midpoint - target_col + row_count, row_count)
        return place(target_row, target_col, depth)

    def depth_device(step):
        return place(row, col, lax.rem(depth + step, depth_count))

    def send(source, target, send_sem, recv_sem, device):
        return pltpu.make_async_remote_copy(
            src_ref=source, dst_ref=target, send_sem=send_sem, recv_sem=recv_sem,
            device_id=device, device_id_type=MESH,
        )

    def home_copy(step):
        return send(
            x_ref.at[0], home.at[step],
            home_send.at[step], home_recv.at[step], home_device(step),
        )

    def home_rows_copy(step):
        return send(
            rows_hbm.at[0], home_rows.at[step],
            row_send.at[0, step], row_recv.at[0, step], home_device(step),
        )

    def partner_copy(step, chunk):
        return send(
            x_ref.at[0, :, :, pl.ds(chunk * sub, sub)], partner[chunk].at[step],
            partner_send.at[step, chunk], partner_recv.at[step, chunk],
            partner_device(step),
        )

    def partner_rows_copy(step):
        return send(
            rows_hbm.at[0], partner_rows.at[step],
            row_send.at[1, step], row_recv.at[1, step], partner_device(step),
        )

    def pos_copy(step):
        return send(
            pos_vmem.at[0], pos_vmem.at[step],
            pos_send.at[step], pos_recv.at[step], depth_device(step),
        )

    def sum_copy(step, chunk):
        columns = pl.ds(chunk * sub, sub)
        return send(
            send_parts.at[step, columns], recv_parts.at[step, columns],
            sum_send.at[step, chunk], sum_recv.at[step, chunk], depth_device(step),
        )

    def sends_partner(step):
        return lax.rem(col + step, col_count) != midpoint

    for step in range(col_count):
        pl.when(sends_partner(step))(lambda: partner_copy(step, 0).start())
    loads[2].wait()
    for step in range(1, depth_count):
        pos_copy(step).start()
    for step in range(col_count):
        if step:
            home_rows_copy(step).start()
            home_copy(step).start()
        pl.when(sends_partner(step))(lambda: partner_rows_copy(step).start())
    for chunk in range(1, chunks):
        for step in range(col_count):
            pl.when(sends_partner(step))(lambda: partner_copy(step, chunk).start())

    for copy in loads[:2]:
        copy.wait()
    for step in range(1, col_count):
        home_rows_copy(step).wait_recv()
    to_smem = pltpu.make_async_copy(home_rows, rows_smem.at[0], local_sem.at[3])
    to_smem.start()
    for step in range(1, depth_count):
        pos_copy(step).wait_recv()
    positions = [
        pos_vmem[(depth_count - step) % depth_count, 0, 0] for step in range(depth_count)
    ]
    to_smem.wait()
    for step in range(1, col_count):
        home_copy(step).wait_recv()

    def find(side, block_row):
        places = []
        for index in range(col_count):
            for column in range(width):
                slot = jnp.int32(0)
                found = jnp.int32(0)
                for number in range(slots):
                    match = rows_smem[side, index, column, number] == block_row
                    slot = jnp.where(match, number, slot)
                    found = jnp.where(match, 1, found)
                places.append((index, column, slot, found))
        return places

    def pick(places, read):
        blocks = []
        for index, column, slot, found in places:
            block = read(index, column, slot)
            blocks.append(jnp.where(found > 0, block, jnp.zeros_like(block)))
        return jnp.concatenate(blocks, axis=1)

    steps = list(range(1, depth_count)) + [0]
    for step in steps:
        left[step] = pick(
            find(0, lax.div(positions[step], group_rows)),
            lambda index, column, slot: home[index, column, slot],
        )

    def find_all(side):
        return [find(side, lax.rem(positions[step], group_rows)) for step in range(depth_count)]

    def tile(places, read, chunk):
        columns = slice(chunk * sub, (chunk + 1) * sub)
        totals = [product(pick(places[step], read), left[step]) for step in steps]
        for step, total in zip(steps, totals):
            send_parts[step, columns] = total
        for step in range(1, depth_count):
            sum_copy(step, chunk).start()

    @pl.when(has_partner)
    def _():
        for step in range(col_count):
            partner_rows_copy(step).wait_recv()
        moved = pltpu.make_async_copy(partner_rows, rows_smem.at[1], local_sem.at[4])
        moved.start()
        moved.wait()
        places = find_all(1)
        for chunk in range(chunks):
            for step in range(col_count):
                partner_copy(step, chunk).wait_recv()
            tile(places, lambda at, column, slot: partner[chunk][at, column, slot], chunk)

    @pl.when(jnp.logical_not(has_partner))
    def _():
        places = find_all(0)
        for chunk in range(chunks):
            columns = slice(chunk * sub, (chunk + 1) * sub)
            tile(places, lambda at, column, slot: home[at, column, slot, columns], chunk)

    for chunk in range(chunks):
        columns = slice(chunk * sub, (chunk + 1) * sub)
        total = send_parts[0, columns]
        for step in range(1, depth_count):
            sum_copy(step, chunk).wait_recv()
            total = total + recv_parts[step, columns]
        send_parts[0, columns] = total
    out_ref[0, 0, 0] = send_parts[0].T.astype(out_ref.dtype)

    for step in range(col_count):
        if step:
            home_copy(step).wait_send()
            home_rows_copy(step).wait_send()
        pl.when(sends_partner(step))(lambda: partner_rows_copy(step).wait_send())
    for step in range(1, depth_count):
        pos_copy(step).wait_send()
    for chunk in range(chunks):
        for step in range(col_count):
            pl.when(sends_partner(step))(lambda: partner_copy(step, chunk).wait_send())
        for step in range(1, depth_count):
            sum_copy(step, chunk).wait_send()


def on_device(sizes, x_vals, x_rows, out_block):
    row_count, col_count, depth_count = sizes
    _, width, slots, size, _ = x_vals.shape
    sub = size // CHUNKS
    block_set = (col_count, width, slots)
    dma = pltpu.SemaphoreType.DMA
    return pl.pallas_call(
        functools.partial(kernel, sizes),
        out_shape=jax.ShapeDtypeStruct(out_block.shape + (size, size), jnp.bfloat16),
        in_specs=[
            pl.BlockSpec(memory_space=pl.ANY),
            pl.BlockSpec(memory_space=pl.ANY),
            pl.BlockSpec(memory_space=pl.ANY),
        ],
        out_specs=pl.BlockSpec(memory_space=pltpu.VMEM),
        scratch_shapes=[
            pltpu.VMEM(block_set + (size, size), x_vals.dtype),
            pltpu.VMEM(block_set, jnp.int32),
            tuple(pltpu.VMEM(block_set + (sub, size), x_vals.dtype) for _ in range(CHUNKS)),
            pltpu.VMEM(block_set, jnp.int32),
            pltpu.SMEM((2,) + block_set, jnp.int32),
            pltpu.VMEM((depth_count,) + out_block.shape[1:], jnp.int32),
            pltpu.VMEM((depth_count, size, col_count * width * size), x_vals.dtype),
            pltpu.VMEM((depth_count, size, size), jnp.float32),
            pltpu.VMEM((depth_count, size, size), jnp.float32),
            dma((5,)),
            dma((col_count,)),
            dma((col_count,)),
            dma((col_count, CHUNKS)),
            dma((col_count, CHUNKS)),
            dma((2, col_count)),
            dma((2, col_count)),
            dma((depth_count,)),
            dma((depth_count,)),
            dma((depth_count, CHUNKS)),
            dma((depth_count, CHUNKS)),
        ],
        compiler_params=pltpu.CompilerParams(
            collective_id=0, has_side_effects=True, vmem_limit_bytes=VMEM_LIMIT
        ),
    )(x_rows, out_block, x_vals)


def solution(mesh):
    sizes = tuple(mesh.shape[name] for name in ("row", "col", "depth"))
    in_specs = (
        P("row", ("col", "depth"), None, None, None),
        P("row", ("col", "depth"), None),
        P("row", "col", "depth"),
    )
    out_specs = P("row", "col", "depth", None, None)
    return jax.shard_map(
        functools.partial(on_device, sizes),
        mesh=mesh, in_specs=in_specs, out_specs=out_specs, check_vma=False,
    )
```

```python
import functools

import jax
import jax.numpy as jnp
from jax import lax
from jax.experimental import pallas as pl
from jax.experimental.pallas import tpu as pltpu
from jax.sharding import PartitionSpec as P

MESH = pl.DeviceIdType.MESH
CHUNKS = 4
VMEM_LIMIT = 55072 * 1024


def product(left, right):
    return lax.dot_general(
        left, right, (((1,), (1,)), ((), ())), preferred_element_type=jnp.float32
    )


def kernel(
    sizes, rows_hbm, pos_ref, x_ref, out_ref,
    rows_ref, raw, home, partner, pos_vmem, left, send_parts, recv_parts,
    local_sem, home_send, home_recv, partner_send, partner_recv,
    pos_send, pos_recv, sum_send, sum_recv,
):
    row_count, col_count, depth_count = sizes
    width, slots, size = x_ref.shape[1], x_ref.shape[2], x_ref.shape[3]
    chunks, group_rows, sub = home.shape[1:4]
    wide = home.shape[4]
    midpoint = col_count // 2
    row, col, depth = (lax.axis_index(name) for name in ("row", "col", "depth"))
    has_partner = col != midpoint

    def place(row_index, col_index, depth_index):
        return {"row": row_index, "col": col_index, "depth": depth_index}

    loads = [
        pltpu.make_async_copy(x_ref.at[0], raw, local_sem.at[0]),
        pltpu.make_async_copy(rows_hbm, rows_ref, local_sem.at[1]),
        pltpu.make_async_copy(pos_ref.at[0], pos_vmem.at[0], local_sem.at[2]),
    ]
    for copy in loads:
        copy.start()

    barrier = pltpu.get_barrier_semaphore()

    def greet(device):
        pl.semaphore_signal(barrier, inc=1, device_id=device, device_id_type=MESH)

    for step in range(1, col_count):
        greet(place(row, lax.rem(col + step, col_count), depth))
    for step in range(1, depth_count):
        greet(place(row, col, lax.rem(depth + step, depth_count)))

    @pl.when(has_partner)
    def _():
        source_row = lax.rem(row + col - midpoint + row_count, row_count)
        for step in range(col_count):
            greet(place(source_row, lax.rem(col + step, col_count), depth))

    for copy in loads:
        copy.wait()
    for column in range(width):
        for block_row in range(group_rows):
            slot = jnp.int32(0)
            found = jnp.int32(0)
            for index in range(slots):
                match = rows_ref[0, column, index] == block_row
                slot = jnp.where(match, index, slot)
                found = jnp.where(match, 1, found)
            block = raw[column, slot]
            block = jnp.where(found > 0, block, jnp.zeros_like(block))
            home[0, :, block_row, :, column * size:(column + 1) * size] = block.reshape(
                chunks, sub, size
            )

    pl.semaphore_wait(barrier, 2 * (col_count - 1) + depth_count - 1)

    def home_copy(step):
        return pltpu.make_async_remote_copy(
            src_ref=home.at[0],
            dst_ref=home.at[step],
            send_sem=home_send.at[step],
            recv_sem=home_recv.at[step],
            device_id=place(row, lax.rem(col + step, col_count), depth),
            device_id_type=MESH,
        )

    def partner_copy(step, chunk):
        target_col = lax.rem(col + step, col_count)
        target_row = lax.rem(row + midpoint - target_col + row_count, row_count)
        return pltpu.make_async_remote_copy(
            src_ref=home.at[0, chunk],
            dst_ref=partner[chunk].at[step],
            send_sem=partner_send.at[step, chunk],
            recv_sem=partner_recv.at[step, chunk],
            device_id=place(target_row, target_col, depth),
            device_id_type=MESH,
        )

    def pos_copy(step):
        return pltpu.make_async_remote_copy(
            src_ref=pos_vmem.at[0],
            dst_ref=pos_vmem.at[step],
            send_sem=pos_send.at[step],
            recv_sem=pos_recv.at[step],
            device_id=place(row, col, lax.rem(depth + step, depth_count)),
            device_id_type=MESH,
        )

    def sum_copy(step, chunk):
        columns = pl.ds(chunk * sub, sub)
        return pltpu.make_async_remote_copy(
            src_ref=send_parts.at[step, columns],
            dst_ref=recv_parts.at[step, columns],
            send_sem=sum_send.at[step, chunk],
            recv_sem=sum_recv.at[step, chunk],
            device_id=place(row, col, lax.rem(depth + step, depth_count)),
            device_id_type=MESH,
        )

    def sends_partner(step):
        return lax.rem(col + step, col_count) != midpoint

    for step in range(1, depth_count):
        pos_copy(step).start()
    for chunk in range(chunks):
        for step in range(col_count):
            pl.when(sends_partner(step))(lambda: partner_copy(step, chunk).start())
            if step and not chunk:
                home_copy(step).start()
    for step in range(1, depth_count):
        pos_copy(step).wait_recv()
    positions = [pos_vmem[step, 0, 0] for step in range(depth_count)]
    for step in range(1, col_count):
        home_copy(step).wait_recv()

    steps = list(range(1, depth_count)) + [0]
    for step in steps:
        left_row = lax.div(positions[(depth_count - step) % depth_count], group_rows)
        left[step] = jnp.concatenate(
            [home[index, :, left_row].reshape(size, wide) for index in range(col_count)], axis=1
        )

    def tile(read, chunk):
        columns = slice(chunk * sub, (chunk + 1) * sub)
        totals = []
        for step in steps:
            right_row = lax.rem(positions[(depth_count - step) % depth_count], group_rows)
            right = jnp.concatenate(
                [read(index, chunk, right_row) for index in range(col_count)], axis=1
            )
            totals.append(product(right, left[step]))
        for step, total in zip(steps, totals):
            send_parts[step, columns] = total
        for step in range(1, depth_count):
            sum_copy(step, chunk).start()

    @pl.when(has_partner)
    def _():
        for chunk in range(chunks):
            for step in range(col_count):
                partner_copy(step, chunk).wait_recv()
            tile(lambda index, part, block_row: partner[part][index, block_row], chunk)

    @pl.when(jnp.logical_not(has_partner))
    def _():
        for chunk in range(chunks):
            tile(lambda index, part, block_row: home[index, part, block_row], chunk)

    for chunk in range(chunks):
        columns = slice(chunk * sub, (chunk + 1) * sub)
        total = send_parts[0, columns]
        for step in range(1, depth_count):
            sum_copy(step, chunk).wait_recv()
            total = total + recv_parts[step, columns]
        send_parts[0, columns] = total
    out_ref[0, 0, 0] = send_parts[0].T.astype(out_ref.dtype)

    for step in range(1, col_count):
        home_copy(step).wait_send()
    for step in range(1, depth_count):
        pos_copy(step).wait_send()
    for chunk in range(chunks):
        for step in range(col_count):
            pl.when(sends_partner(step))(lambda: partner_copy(step, chunk).wait_send())
        for step in range(1, depth_count):
            sum_copy(step, chunk).wait_send()


def on_device(sizes, x_vals, x_rows, out_block):
    row_count, col_count, depth_count = sizes
    _, width, slots, size, _ = x_vals.shape
    group_rows = width * col_count * depth_count // row_count
    staged = (col_count, CHUNKS, group_rows, size // CHUNKS, width * size)
    dma = pltpu.SemaphoreType.DMA
    return pl.pallas_call(
        functools.partial(kernel, sizes),
        out_shape=jax.ShapeDtypeStruct(out_block.shape + (size, size), jnp.bfloat16),
        in_specs=[
            pl.BlockSpec(memory_space=pl.ANY),
            pl.BlockSpec(memory_space=pl.ANY),
            pl.BlockSpec(memory_space=pl.ANY),
        ],
        out_specs=pl.BlockSpec(memory_space=pltpu.VMEM),
        scratch_shapes=[
            pltpu.SMEM(x_rows.shape, jnp.int32),
            pltpu.VMEM((width, slots, size, size), x_vals.dtype),
            pltpu.VMEM(staged, x_vals.dtype),
            tuple(pltpu.VMEM(staged[:1] + staged[2:], x_vals.dtype) for _ in range(CHUNKS)),
            pltpu.VMEM((depth_count,) + out_block.shape[1:], jnp.int32),
            pltpu.VMEM((depth_count, size, col_count * width * size), x_vals.dtype),
            pltpu.VMEM((depth_count, size, size), jnp.float32),
            pltpu.VMEM((depth_count, size, size), jnp.float32),
            dma((3,)),
            dma((col_count,)),
            dma((col_count,)),
            dma((col_count, CHUNKS)),
            dma((col_count, CHUNKS)),
            dma((depth_count,)),
            dma((depth_count,)),
            dma((depth_count, CHUNKS)),
            dma((depth_count, CHUNKS)),
        ],
        compiler_params=pltpu.CompilerParams(
            collective_id=0, has_side_effects=True, vmem_limit_bytes=VMEM_LIMIT
        ),
    )(x_rows, out_block, x_vals)


def solution(mesh):
    sizes = tuple(mesh.shape[name] for name in ("row", "col", "depth"))
    in_specs = (
        P("row", ("col", "depth"), None, None, None),
        P("row", ("col", "depth"), None),
        P("row", "col", "depth"),
    )
    out_specs = P("row", "col", "depth", None, None)
    return jax.shard_map(
        functools.partial(on_device, sizes),
        mesh=mesh, in_specs=in_specs, out_specs=out_specs, check_vma=False,
    )
```

```python
import functools

import jax
import jax.numpy as jnp
from jax import lax
from jax.experimental import pallas as pl
from jax.experimental.pallas import tpu as pltpu
from jax.sharding import PartitionSpec as P

MESH = pl.DeviceIdType.MESH
CHUNKS = 4
VMEM_LIMIT = 55072 * 1024


def product(left, right):
    return lax.dot_general(
        left, right, (((1,), (1,)), ((), ())), preferred_element_type=jnp.float32
    )


def kernel(
    sizes, rows_hbm, pos_ref, x_ref, out_ref,
    rows_ref, raw, home, partner, pos_vmem, left, send_parts, recv_parts,
    local_sem, home_send, home_recv, partner_send, partner_recv,
    pos_send, pos_recv, sum_send, sum_recv,
):
    row_count, col_count, depth_count = sizes
    width, slots, size = x_ref.shape[1], x_ref.shape[2], x_ref.shape[3]
    chunks, group_rows, sub = home.shape[1:4]
    wide = home.shape[4]
    midpoint = col_count // 2
    row, col, depth = (lax.axis_index(name) for name in ("row", "col", "depth"))
    has_partner = col != midpoint

    def place(row_index, col_index, depth_index):
        return {"row": row_index, "col": col_index, "depth": depth_index}

    loads = [
        pltpu.make_async_copy(x_ref.at[0], raw, local_sem.at[0]),
        pltpu.make_async_copy(rows_hbm, rows_ref, local_sem.at[1]),
        pltpu.make_async_copy(pos_ref.at[0], pos_vmem.at[0], local_sem.at[2]),
    ]
    for copy in loads:
        copy.start()

    barrier = pltpu.get_barrier_semaphore()

    def greet(device):
        pl.semaphore_signal(barrier, inc=1, device_id=device, device_id_type=MESH)

    for step in range(1, col_count):
        greet(place(row, lax.rem(col + step, col_count), depth))
    for step in range(1, depth_count):
        greet(place(row, col, lax.rem(depth + step, depth_count)))

    @pl.when(has_partner)
    def _():
        source_row = lax.rem(row + col - midpoint + row_count, row_count)
        for step in range(col_count):
            greet(place(source_row, lax.rem(col + step, col_count), depth))

    for copy in loads:
        copy.wait()
    places = []
    for column in range(width):
        for block_row in range(group_rows):
            slot = jnp.int32(0)
            found = jnp.int32(0)
            for index in range(slots):
                match = rows_ref[0, column, index] == block_row
                slot = jnp.where(match, index, slot)
                found = jnp.where(match, 1, found)
            places.append((column, block_row, slot, found))

    pl.semaphore_wait(barrier, 2 * (col_count - 1) + depth_count - 1)

    def home_copy(step):
        return pltpu.make_async_remote_copy(
            src_ref=home.at[0],
            dst_ref=home.at[step],
            send_sem=home_send.at[step],
            recv_sem=home_recv.at[step],
            device_id=place(row, lax.rem(col + step, col_count), depth),
            device_id_type=MESH,
        )

    def partner_copy(step, chunk):
        target_col = lax.rem(col + step, col_count)
        target_row = lax.rem(row + midpoint - target_col + row_count, row_count)
        return pltpu.make_async_remote_copy(
            src_ref=home.at[0, chunk],
            dst_ref=partner[chunk].at[step],
            send_sem=partner_send.at[step, chunk],
            recv_sem=partner_recv.at[step, chunk],
            device_id=place(target_row, target_col, depth),
            device_id_type=MESH,
        )

    def pos_copy(step):
        return pltpu.make_async_remote_copy(
            src_ref=pos_vmem.at[0],
            dst_ref=pos_vmem.at[step],
            send_sem=pos_send.at[step],
            recv_sem=pos_recv.at[step],
            device_id=place(row, col, lax.rem(depth + step, depth_count)),
            device_id_type=MESH,
        )

    def sum_copy(step, chunk):
        columns = pl.ds(chunk * sub, sub)
        return pltpu.make_async_remote_copy(
            src_ref=send_parts.at[step, columns],
            dst_ref=recv_parts.at[step, columns],
            send_sem=sum_send.at[step, chunk],
            recv_sem=sum_recv.at[step, chunk],
            device_id=place(row, col, lax.rem(depth + step, depth_count)),
            device_id_type=MESH,
        )

    def sends_partner(step):
        return lax.rem(col + step, col_count) != midpoint

    for step in range(1, depth_count):
        pos_copy(step).start()
    for chunk in range(chunks):
        lines = slice(chunk * sub, (chunk + 1) * sub)
        for column, block_row, slot, found in places:
            block = raw[column, slot, lines]
            home[0, chunk, block_row, :, column * size:(column + 1) * size] = jnp.where(
                found > 0, block, jnp.zeros_like(block)
            )
        for step in range(col_count):
            pl.when(sends_partner(step))(lambda: partner_copy(step, chunk).start())
    for step in range(1, col_count):
        home_copy(step).start()

    for step in range(1, depth_count):
        pos_copy(step).wait_recv()
    positions = [pos_vmem[step, 0, 0] for step in range(depth_count)]
    for step in range(1, col_count):
        home_copy(step).wait_recv()

    steps = list(range(1, depth_count)) + [0]
    for step in steps:
        left_row = lax.div(positions[(depth_count - step) % depth_count], group_rows)
        left[step] = jnp.concatenate(
            [home[index, :, left_row].reshape(size, wide) for index in range(col_count)], axis=1
        )

    def tile(read, chunk):
        columns = slice(chunk * sub, (chunk + 1) * sub)
        totals = []
        for step in steps:
            right_row = lax.rem(positions[(depth_count - step) % depth_count], group_rows)
            right = jnp.concatenate(
                [read(index, chunk, right_row) for index in range(col_count)], axis=1
            )
            totals.append(product(right, left[step]))
        for step, total in zip(steps, totals):
            send_parts[step, columns] = total
        for step in range(1, depth_count):
            sum_copy(step, chunk).start()

    @pl.when(has_partner)
    def _():
        for chunk in range(chunks):
            for step in range(col_count):
                partner_copy(step, chunk).wait_recv()
            tile(lambda index, part, block_row: partner[part][index, block_row], chunk)

    @pl.when(jnp.logical_not(has_partner))
    def _():
        for chunk in range(chunks):
            tile(lambda index, part, block_row: home[index, part, block_row], chunk)

    for chunk in range(chunks):
        columns = slice(chunk * sub, (chunk + 1) * sub)
        total = send_parts[0, columns]
        for step in range(1, depth_count):
            sum_copy(step, chunk).wait_recv()
            total = total + recv_parts[step, columns]
        send_parts[0, columns] = total
    out_ref[0, 0, 0] = send_parts[0].T.astype(out_ref.dtype)

    for step in range(1, col_count):
        home_copy(step).wait_send()
    for step in range(1, depth_count):
        pos_copy(step).wait_send()
    for chunk in range(chunks):
        for step in range(col_count):
            pl.when(sends_partner(step))(lambda: partner_copy(step, chunk).wait_send())
        for step in range(1, depth_count):
            sum_copy(step, chunk).wait_send()


def on_device(sizes, x_vals, x_rows, out_block):
    row_count, col_count, depth_count = sizes
    _, width, slots, size, _ = x_vals.shape
    group_rows = width * col_count * depth_count // row_count
    staged = (col_count, CHUNKS, group_rows, size // CHUNKS, width * size)
    dma = pltpu.SemaphoreType.DMA
    return pl.pallas_call(
        functools.partial(kernel, sizes),
        out_shape=jax.ShapeDtypeStruct(out_block.shape + (size, size), jnp.bfloat16),
        in_specs=[
            pl.BlockSpec(memory_space=pl.ANY),
            pl.BlockSpec(memory_space=pl.ANY),
            pl.BlockSpec(memory_space=pl.ANY),
        ],
        out_specs=pl.BlockSpec(memory_space=pltpu.VMEM),
        scratch_shapes=[
            pltpu.SMEM(x_rows.shape, jnp.int32),
            pltpu.VMEM((width, slots, size, size), x_vals.dtype),
            pltpu.VMEM(staged, x_vals.dtype),
            tuple(pltpu.VMEM(staged[:1] + staged[2:], x_vals.dtype) for _ in range(CHUNKS)),
            pltpu.VMEM((depth_count,) + out_block.shape[1:], jnp.int32),
            pltpu.VMEM((depth_count, size, col_count * width * size), x_vals.dtype),
            pltpu.VMEM((depth_count, size, size), jnp.float32),
            pltpu.VMEM((depth_count, size, size), jnp.float32),
            dma((3,)),
            dma((col_count,)),
            dma((col_count,)),
            dma((col_count, CHUNKS)),
            dma((col_count, CHUNKS)),
            dma((depth_count,)),
            dma((depth_count,)),
            dma((depth_count, CHUNKS)),
            dma((depth_count, CHUNKS)),
        ],
        compiler_params=pltpu.CompilerParams(
            collective_id=0, has_side_effects=True, vmem_limit_bytes=VMEM_LIMIT
        ),
    )(x_rows, out_block, x_vals)


def solution(mesh):
    sizes = tuple(mesh.shape[name] for name in ("row", "col", "depth"))
    in_specs = (
        P("row", ("col", "depth"), None, None, None),
        P("row", ("col", "depth"), None),
        P("row", "col", "depth"),
    )
    out_specs = P("row", "col", "depth", None, None)
    return jax.shard_map(
        functools.partial(on_device, sizes),
        mesh=mesh, in_specs=in_specs, out_specs=out_specs, check_vma=False,
    )
```

```python
import functools

import jax
import jax.numpy as jnp
from jax import lax
from jax.experimental import pallas as pl
from jax.experimental.pallas import tpu as pltpu
from jax.sharding import PartitionSpec as P

MESH = pl.DeviceIdType.MESH
CHUNKS = 2
VMEM_LIMIT = 55072 * 1024


def product(left, right):
    return lax.dot_general(
        left, right, (((1,), (1,)), ((), ())), preferred_element_type=jnp.float32
    )


def kernel(
    sizes, rows_hbm, pos_ref, x_ref, out_ref,
    rows_ref, raw, home, partner, pos_vmem, left, send_parts, recv_parts,
    local_sem, home_send, home_recv, partner_send, partner_recv,
    pos_send, pos_recv, sum_send, sum_recv,
):
    row_count, col_count, depth_count = sizes
    width, slots, size = x_ref.shape[1], x_ref.shape[2], x_ref.shape[3]
    chunks, group_rows, sub = home.shape[1:4]
    wide = home.shape[4]
    midpoint = col_count // 2
    row, col, depth = (lax.axis_index(name) for name in ("row", "col", "depth"))
    has_partner = col != midpoint

    def place(row_index, col_index, depth_index):
        return {"row": row_index, "col": col_index, "depth": depth_index}

    loads = [
        pltpu.make_async_copy(x_ref.at[0], raw, local_sem.at[0]),
        pltpu.make_async_copy(rows_hbm, rows_ref, local_sem.at[1]),
        pltpu.make_async_copy(pos_ref.at[0], pos_vmem.at[0], local_sem.at[2]),
    ]
    for copy in loads:
        copy.start()

    barrier = pltpu.get_barrier_semaphore()

    def greet(device):
        pl.semaphore_signal(barrier, inc=1, device_id=device, device_id_type=MESH)

    for step in range(1, col_count):
        greet(place(row, lax.rem(col + step, col_count), depth))
    for step in range(1, depth_count):
        greet(place(row, col, lax.rem(depth + step, depth_count)))

    @pl.when(has_partner)
    def _():
        source_row = lax.rem(row + col - midpoint + row_count, row_count)
        for step in range(col_count):
            greet(place(source_row, lax.rem(col + step, col_count), depth))

    for copy in loads:
        copy.wait()
    places = []
    for column in range(width):
        for block_row in range(group_rows):
            slot = jnp.int32(0)
            found = jnp.int32(0)
            for index in range(slots):
                match = rows_ref[0, column, index] == block_row
                slot = jnp.where(match, index, slot)
                found = jnp.where(match, 1, found)
            places.append((column, block_row, slot, found))

    pl.semaphore_wait(barrier, 2 * (col_count - 1) + depth_count - 1)

    def home_copy(step):
        return pltpu.make_async_remote_copy(
            src_ref=home.at[0],
            dst_ref=home.at[step],
            send_sem=home_send.at[step],
            recv_sem=home_recv.at[step],
            device_id=place(row, lax.rem(col + step, col_count), depth),
            device_id_type=MESH,
        )

    def partner_copy(step, chunk):
        target_col = lax.rem(col + step, col_count)
        target_row = lax.rem(row + midpoint - target_col + row_count, row_count)
        return pltpu.make_async_remote_copy(
            src_ref=home.at[0, chunk],
            dst_ref=partner[chunk].at[step],
            send_sem=partner_send.at[step, chunk],
            recv_sem=partner_recv.at[step, chunk],
            device_id=place(target_row, target_col, depth),
            device_id_type=MESH,
        )

    def pos_copy(step):
        return pltpu.make_async_remote_copy(
            src_ref=pos_vmem.at[0],
            dst_ref=pos_vmem.at[step],
            send_sem=pos_send.at[step],
            recv_sem=pos_recv.at[step],
            device_id=place(row, col, lax.rem(depth + step, depth_count)),
            device_id_type=MESH,
        )

    def sum_copy(step, chunk):
        columns = pl.ds(chunk * sub, sub)
        return pltpu.make_async_remote_copy(
            src_ref=send_parts.at[step, columns],
            dst_ref=recv_parts.at[step, columns],
            send_sem=sum_send.at[step, chunk],
            recv_sem=sum_recv.at[step, chunk],
            device_id=place(row, col, lax.rem(depth + step, depth_count)),
            device_id_type=MESH,
        )

    def sends_partner(step):
        return lax.rem(col + step, col_count) != midpoint

    for step in range(1, depth_count):
        pos_copy(step).start()
    for chunk in range(chunks):
        lines = slice(chunk * sub, (chunk + 1) * sub)
        for column, block_row, slot, found in places:
            block = raw[column, slot, lines]
            home[0, chunk, block_row, :, column * size:(column + 1) * size] = jnp.where(
                found > 0, block, jnp.zeros_like(block)
            )
        for step in range(col_count):
            pl.when(sends_partner(step))(lambda: partner_copy(step, chunk).start())
    for step in range(1, col_count):
        home_copy(step).start()

    for step in range(1, depth_count):
        pos_copy(step).wait_recv()
    positions = [pos_vmem[step, 0, 0] for step in range(depth_count)]
    for step in range(1, col_count):
        home_copy(step).wait_recv()

    steps = list(range(1, depth_count)) + [0]
    for step in steps:
        left_row = lax.div(positions[(depth_count - step) % depth_count], group_rows)
        left[step] = jnp.concatenate(
            [home[index, :, left_row].reshape(size, wide) for index in range(col_count)], axis=1
        )

    def tile(read, chunk):
        columns = slice(chunk * sub, (chunk + 1) * sub)
        totals = []
        for step in steps:
            right_row = lax.rem(positions[(depth_count - step) % depth_count], group_rows)
            right = jnp.concatenate(
                [read(index, chunk, right_row) for index in range(col_count)], axis=1
            )
            totals.append(product(right, left[step]))
        for step, total in zip(steps, totals):
            send_parts[step, columns] = total
        for step in range(1, depth_count):
            sum_copy(step, chunk).start()

    @pl.when(has_partner)
    def _():
        for chunk in range(chunks):
            for step in range(col_count):
                partner_copy(step, chunk).wait_recv()
            tile(lambda index, part, block_row: partner[part][index, block_row], chunk)

    @pl.when(jnp.logical_not(has_partner))
    def _():
        for chunk in range(chunks):
            tile(lambda index, part, block_row: home[index, part, block_row], chunk)

    for chunk in range(chunks):
        columns = slice(chunk * sub, (chunk + 1) * sub)
        total = send_parts[0, columns]
        for step in range(1, depth_count):
            sum_copy(step, chunk).wait_recv()
            total = total + recv_parts[step, columns]
        send_parts[0, columns] = total
    out_ref[0, 0, 0] = send_parts[0].T.astype(out_ref.dtype)

    for step in range(1, col_count):
        home_copy(step).wait_send()
    for step in range(1, depth_count):
        pos_copy(step).wait_send()
    for chunk in range(chunks):
        for step in range(col_count):
            pl.when(sends_partner(step))(lambda: partner_copy(step, chunk).wait_send())
        for step in range(1, depth_count):
            sum_copy(step, chunk).wait_send()


def on_device(sizes, x_vals, x_rows, out_block):
    row_count, col_count, depth_count = sizes
    _, width, slots, size, _ = x_vals.shape
    group_rows = width * col_count * depth_count // row_count
    staged = (col_count, CHUNKS, group_rows, size // CHUNKS, width * size)
    dma = pltpu.SemaphoreType.DMA
    return pl.pallas_call(
        functools.partial(kernel, sizes),
        out_shape=jax.ShapeDtypeStruct(out_block.shape + (size, size), jnp.bfloat16),
        in_specs=[
            pl.BlockSpec(memory_space=pl.ANY),
            pl.BlockSpec(memory_space=pl.ANY),
            pl.BlockSpec(memory_space=pl.ANY),
        ],
        out_specs=pl.BlockSpec(memory_space=pltpu.VMEM),
        scratch_shapes=[
            pltpu.SMEM(x_rows.shape, jnp.int32),
            pltpu.VMEM((width, slots, size, size), x_vals.dtype),
            pltpu.VMEM(staged, x_vals.dtype),
            tuple(pltpu.VMEM(staged[:1] + staged[2:], x_vals.dtype) for _ in range(CHUNKS)),
            pltpu.VMEM((depth_count,) + out_block.shape[1:], jnp.int32),
            pltpu.VMEM((depth_count, size, col_count * width * size), x_vals.dtype),
            pltpu.VMEM((depth_count, size, size), jnp.float32),
            pltpu.VMEM((depth_count, size, size), jnp.float32),
            dma((3,)),
            dma((col_count,)),
            dma((col_count,)),
            dma((col_count, CHUNKS)),
            dma((col_count, CHUNKS)),
            dma((depth_count,)),
            dma((depth_count,)),
            dma((depth_count, CHUNKS)),
            dma((depth_count, CHUNKS)),
        ],
        compiler_params=pltpu.CompilerParams(
            collective_id=0, has_side_effects=True, vmem_limit_bytes=VMEM_LIMIT
        ),
    )(x_rows, out_block, x_vals)


def solution(mesh):
    sizes = tuple(mesh.shape[name] for name in ("row", "col", "depth"))
    in_specs = (
        P("row", ("col", "depth"), None, None, None),
        P("row", ("col", "depth"), None),
        P("row", "col", "depth"),
    )
    out_specs = P("row", "col", "depth", None, None)
    return jax.shard_map(
        functools.partial(on_device, sizes),
        mesh=mesh, in_specs=in_specs, out_specs=out_specs, check_vma=False,
    )
```
